256 devices in a mesh: tm: 16 (over x_lo, y, core), rows: 16 (over x_hi, z).
Axes of the slice: x: 4 (x_hi: 2, x_lo: 2; x = x_hi * 2 + x_lo), y: 4, z: 8, core: 2. Of those that a mesh axis runs over, the one named last changes fastest.
Arguments:
- latents: bfloat16 [48, 16, 16, 768], P('tm', 'rows'), may hold values from -105 to 105
- first_gain: float32 [768], replicated, may hold values from 0.1 to 1.9
- first_bias: float32 [768], replicated, may hold values from -3 to 3
- second_gain: float32 [768], replicated, may hold values from 0.1 to 1.9
- second_bias: float32 [768], replicated, may hold values from -3 to 3
- first_kernel: bfloat16 [3, 3, 3, 768, 768], P(None, None, None, 'rows'), may hold values from -0.0390625 to 0.0390625
- second_kernel: bfloat16 [3, 3, 3, 768, 768], P(None, None, None, 'rows'), may hold values from -0.0390625 to 0.0390625
- expand_kernel: bfloat16 [768, 6144], P(None, 'rows'), may hold values from -0.21875 to 0.21875
Outputs:
- decoded: bfloat16 [144, 32, 32, 512], P('tm', 'rows')
The draws below stay inside these ranges and needn't reach their ends.
All inputs are finite; a program needn't handle non-finite values.
Results may differ from the reference program's by a relative error of at most 0.0051.
Values may be sent and summed in bfloat16 or wider, within the bound.
A program may use at most 128 MiB of HBM per device.

```python
import jax
import jax.numpy as jnp
from jax import lax

CH = 768
CO = 512
GROUPS = 32
W = 16
NT = 48
NR = 16


def draw_latents(key, part):
    key = jax.random.fold_in(key, 11)
    key_base, key_row, key_chan = jax.random.split(key, 3)
    frame_index = jnp.arange(NT, dtype=jnp.float32)
    frame_scale = jnp.exp(jnp.log(3.0) * frame_index / max(NT - 1, 1))
    row_scale = jnp.exp(jax.random.uniform(key_row, (NR,), minval=0.0, maxval=jnp.log(3.5)))
    chan_scale = jnp.exp(jax.random.uniform(key_chan, (CH,), minval=0.0, maxval=jnp.log(10.0)))
    base = jax.random.truncated_normal(key_base, -4.0, 4.0, (NT, NR, W, CH))
    scale = frame_scale[:, None, None, None] * row_scale[None, :, None, None] * chan_scale[None, None, None, :] * 0.25
    return (base * scale).astype(jnp.bfloat16)


def shard_levels(own_key, shape, shards, least, high):
    def one(axis_at, parts):
        draws = jax.random.uniform(jax.random.fold_in(jax.random.fold_in(own_key, 6), axis_at), (parts,), jnp.float32, least / len(shards), high / len(shards))
        return jnp.repeat(jnp.exp(draws), shape[axis_at] // parts).reshape((-1,) + (1,) * (len(shape) - axis_at - 1))

    factor_of = one(*shards[0])
    for cut in shards[1:]:
        factor_of = factor_of * one(*cut)
    return factor_of


def noise(rng, shape, width, bound, pieces=(), kind=jnp.bfloat16):
    result = jax.random.normal(rng, shape, jnp.float32) * width
    if len(pieces) > 0:
        result = shard_levels(rng, shape, pieces, -0.22, 0.18) * result
    return jnp.clip(result, min=-bound, max=bound).astype(kind)


def setup_inputs(seed: int = 0) -> dict:
    streams_of = jax.random.split(jax.random.key(seed), 9)
    return {
        "latents": draw_latents(jax.random.fold_in(streams_of[8], 71), 0),
        "first_gain": jnp.clip(1.0 + 0.18 * jax.random.normal(streams_of[1], (CH,), jnp.float32), 0.1, 1.9),
        "first_bias": noise(streams_of[2], (CH,), 0.5, 3.0, (), jnp.float32),
        "second_gain": jnp.clip(1.0 + 0.18 * jax.random.normal(streams_of[3], (CH,), jnp.float32), 0.1, 1.9),
        "second_bias": noise(streams_of[4], (CH,), 0.5, 3.0, (), jnp.float32),
        "first_kernel": noise(streams_of[5], (3, 3, 3, CH, CH), (27 * CH) ** -0.5, 0.0390625, ((3, 16),)),
        "second_kernel": noise(streams_of[6], (3, 3, 3, CH, CH), (27 * CH) ** -0.5, 0.0390625, ((3, 16),)),
        "expand_kernel": noise(streams_of[7], (CH, 12 * CO), CH ** -0.5, 0.21875, ((1, 16),)),
    }


def group_norm(field, gain, shift_bias):
    values = field.astype(jnp.float32)
    total_count = values.shape[0] * values.shape[1] * values.shape[2] * (CH // GROUPS)
    chan_sums = lax.optimization_barrier(jnp.sum(values, axis=(0, 1, 2)))
    chan_squares = lax.optimization_barrier(jnp.sum(values * values, axis=(0, 1, 2)))
    group_sum = chan_sums.reshape(GROUPS, -1).sum(1)
    group_square = chan_squares.reshape(GROUPS, -1).sum(1)
    average = group_sum / total_count
    spread = group_square / total_count - average * average
    inv_scale = lax.rsqrt(spread + 1e-06)
    chan_average = jnp.repeat(average, CH // GROUPS)
    chan_scale = jnp.repeat(inv_scale, CH // GROUPS)
    normed = (values - chan_average) * chan_scale * gain + shift_bias
    return jax.nn.silu(normed).astype(jnp.bfloat16)

def causal_conv(field, kernel):
    frames_n, rows_n, width_n = (field.shape[0], field.shape[1], field.shape[2])
    padded = jnp.pad(field.astype(jnp.float32), ((2, 0), (1, 1), (1, 1), (0, 0)))
    total = jnp.zeros((frames_n, rows_n, width_n, kernel.shape[3]), jnp.float32)
    for tap_time in range(3):
        for tap_row in range(3):
            for tap_col in range(3):
                window = padded[tap_time:tap_time + frames_n, tap_row:tap_row + rows_n, tap_col:tap_col + width_n]
                total = total + jnp.einsum('thwc,dc->thwd', window, kernel[tap_time, tap_row, tap_col].astype(jnp.float32), precision=lax.Precision.HIGHEST)
    return total

def depth_space(expanded):
    frames_n, rows_n, width_n = (expanded.shape[0], expanded.shape[1], expanded.shape[2])
    out_chan = expanded.shape[3] // 12
    parted = expanded.reshape(frames_n, rows_n, width_n, out_chan, 3, 2, 2)
    moved = parted.transpose(0, 4, 1, 5, 2, 6, 3)
    return moved.reshape(frames_n * 3, rows_n * 2, width_n * 2, out_chan)

def reference(latents, first_gain, first_bias, second_gain, second_bias, first_kernel, second_kernel, expand_kernel):
    act_one = group_norm(latents, first_gain, first_bias)
    hidden_one = causal_conv(act_one, first_kernel).astype(jnp.bfloat16)
    act_two = group_norm(hidden_one, second_gain, second_bias)
    summed = (latents.astype(jnp.float32) + causal_conv(act_two, second_kernel)).astype(jnp.bfloat16)
    expanded = jnp.einsum('thwc,cd->thwd', summed.astype(jnp.float32), expand_kernel.astype(jnp.float32), precision=lax.Precision.HIGHEST).astype(jnp.bfloat16)
    return depth_space(expanded)
```

```python
import jax
import jax.numpy as jnp
from jax import lax
from jax.experimental import pallas as pl
from jax.experimental.pallas import tpu as pltpu
from jax.sharding import PartitionSpec as P

MESH = pl.DeviceIdType.MESH
BF16 = jnp.bfloat16
F32 = jnp.float32
HIGH = lax.Precision.HIGHEST

CH = 768
OWN = 48
FRAMES = 3
PLANE = 256
TAPS = 9 * OWN
COUNT = 48 * 16 * 16 * 24
NT = (((1,), (1,)), ((), ()))


def iota(shape, axis):
    return lax.broadcasted_iota(jnp.int32, shape, axis)


def loop(count, body):
    def step(i, carry):
        body(i)
        return carry

    lax.fori_loop(0, count, step, 0)


def push(src, dst, send_sem, recv_sem, device):
    pltpu.make_async_remote_copy(
        src_ref=src,
        dst_ref=dst,
        send_sem=send_sem,
        recv_sem=recv_sem,
        device_id=device,
        device_id_type=MESH,
    ).start()


def await_recv(ref, sem):
    pltpu.make_async_copy(ref, ref, sem).wait()


def combine(taps):
    lane = iota((OWN, PLANE), 1)
    column = lane & 15
    total = None
    for tap_row in range(3):
        base = tap_row * 3 * OWN
        line = taps[base + OWN : base + 2 * OWN]
        line += jnp.where(column != 0, pltpu.roll(taps[base : base + OWN], 1, 1), 0.0)
        line += jnp.where(
            column != 15, pltpu.roll(taps[base + 2 * OWN : base + 3 * OWN], PLANE - 1, 1), 0.0
        )
        if tap_row == 0:
            line = jnp.where(lane >= 16, pltpu.roll(line, 16, 1), 0.0)
        elif tap_row == 2:
            line = jnp.where(lane < PLANE - 16, pltpu.roll(line, PLANE - 16, 1), 0.0)
        total = line if total is None else total + line
    return total


def silu(value):
    return value * jax.nn.sigmoid(value)


def group_matrix(shape, group_axis):
    channel = iota(shape, 1 - group_axis)
    return ((channel * 2731) >> 16 == iota(shape, group_axis)).astype(F32)


def kernel(
    x_ref,
    gain1_ref,
    bias1_ref,
    gain2_ref,
    bias2_ref,
    w1_hbm,
    w2_hbm,
    ek_ref,
    out_ref,
    w1,
    w2,
    xg,
    act,
    hg,
    ekt,
    taps,
    hid,
    halo_out,
    halo_in,
    stat_rows,
    stat_tm,
    stat_two,
    pack,
    sg,
    sem_w,
    sx_send,
    sx,
    sh_send,
    sh,
    se_send,
    se,
    sstat_send,
    sstat,
    shalo_send,
    shalo,
    sg_send,
    sg_recv,
):
    t = lax.axis_index("tm")
    r = lax.axis_index("rows")
    xh = r // 8
    z = lax.rem(r, 8)
    half = lax.rem(t, 2)

    def slot(other, distance):
        line = 1 - xh if other else xh
        return line * 8 + lax.rem(z + distance + 8, 8)

    up = (t, slot(False, 1))
    down = (t, slot(False, -1))
    partner = (t, slot(True, 0))
    sibling = (t + 1 - 2 * half, r)

    load1 = pltpu.make_async_copy(w1_hbm, w1, sem_w.at[0])
    load2 = pltpu.make_async_copy(w2_hbm, w2, sem_w.at[1])
    load1.start()
    load2.start()

    barrier = pltpu.get_barrier_semaphore()

    def greet(i):
        pl.semaphore_signal(
            barrier, inc=1, device_id=(t, lax.rem(r + 1 + i, 16)), device_id_type=MESH
        )
        pl.semaphore_signal(
            barrier, inc=1, device_id=(lax.rem(t + 1 + i, 16), r), device_id_type=MESH
        )

    loop(15, greet)

    for frame in range(FRAMES):
        xg[pl.ds(pl.multiple_of(frame * PLANE + r * 16, 16), 16)] = x_ref[
            frame * 16 : frame * 16 + 16
        ]
    own = x_ref[...].astype(F32)
    row8 = iota((8, CH), 0)
    sums = jnp.where(
        row8 == 0,
        jnp.sum(own, axis=0, keepdims=True),
        jnp.where(row8 == 1, jnp.sum(own * own, axis=0, keepdims=True), 0.0),
    )
    stat_rows[r] = jnp.dot(
        sums, group_matrix((CH, 128), 1), precision=HIGH, preferred_element_type=F32
    )

    @pl.when(t == 0)
    def _():
        halo_in[...] = jnp.zeros_like(halo_in)

    pl.semaphore_wait(barrier, 30)

    def exchange_rows(i):
        push(
            stat_rows.at[r],
            stat_rows.at[r],
            sstat_send.at[0],
            sstat.at[0],
            (t, lax.rem(r + 1 + i, 16)),
        )

    loop(15, exchange_rows)

    def ring(view, send_sem, sems, after_start):
        def send(which, frame, device):
            ref = view(which, frame)
            push(ref, ref, send_sem, sems.at[which, frame], device)

        def wait(which, frame):
            await_recv(view(which, frame), sems.at[which, frame])

        def start(i):
            frame = FRAMES - 1 - i
            for device in (partner, up, down):
                send(r, frame, device)

        def first(i):
            frame = FRAMES - 1 - i
            which = slot(True, 0)
            wait(which, frame)
            send(which, frame, up)
            send(which, frame, down)

        loop(FRAMES, start)
        after_start()
        loop(FRAMES, first)
        for step in range(1, 5):

            def forward(i, step=step):
                frame = FRAMES - 1 - i
                for other in (False, True):
                    for sign in (-1, 1):
                        last = 4 if (sign == -1) == (not other) else 3
                        if step > last:
                            continue
                        which = slot(other, sign * step)
                        wait(which, frame)
                        if step < last:
                            send(which, frame, up if sign == -1 else down)

            loop(FRAMES, forward)

    def view_x(which, frame):
        return xg.at[pl.ds(pl.multiple_of(frame * PLANE + which * 16, 16), 16)]

    def view_h(which, frame):
        return hg.at[pl.ds(pl.multiple_of(frame * CH + which * OWN, 16), OWN)]

    def exchange_tm():
        await_recv(stat_rows.at[pl.ds(0, 15)], sstat.at[0])
        stat_tm[t] = jnp.sum(stat_rows[...], axis=0)

        def send(i):
            push(
                stat_tm.at[t],
                stat_tm.at[t],
                sstat_send.at[1],
                sstat.at[1],
                (lax.rem(t + 1 + i, 16), r),
            )

        loop(15, send)
        row = iota((384, 384), 0)
        place = (iota((384, 384), 1) == 12 * (row & 31) + (row >> 5)).astype(BF16)
        turned = lax.dot_general(place, ek_ref[...], NT, preferred_element_type=F32).astype(BF16)
        for sub in range(12):
            ekt[sub, pl.ds(pl.multiple_of(r * 32, 32), 32)] = turned[sub * 32 : sub * 32 + 32]

    ring(view_x, sx_send, sx, exchange_tm)

    def view_e(part, which):
        return ekt.at[pl.ds(part * 6, 6), pl.ds(pl.multiple_of(which * 32, 32), 32)]

    def send_e(which, device):
        ref = view_e(half, which)
        push(ref, ref, se_send, se.at[half, which], device)

    def expand_start():
        for device in (up, down, partner):
            send_e(r, device)

    def expand_step(step):
        for sign, last in ((-1, 4), (1, 3)):
            if step > last:
                continue
            which = slot(False, sign * step)
            await_recv(view_e(half, which), se.at[half, which])
            if step < last:
                send_e(which, up if sign == -1 else down)
            send_e(which, partner)
            send_e(which, sibling)

    def expand_across(i):
        which = (1 - xh) * 8 + i
        await_recv(view_e(half, which), se.at[half, which])
        send_e(which, sibling)

    def expand_last(i):
        which = lax.rem(r + 1 + i, 16)
        await_recv(view_e(1 - half, which), se.at[1 - half, which])

    expand_start()

    await_recv(stat_tm.at[pl.ds(0, 15)], sstat.at[1])
    averages = jnp.sum(stat_tm[...], axis=0) * (1.0 / COUNT)
    mean, square = averages[0:1], averages[1:2]
    inverse = lax.rsqrt(square - mean * mean + 1e-06)
    row8 = iota((8, 128), 0)
    spreads = jnp.where(row8 == 0, mean, jnp.where(row8 == 1, inverse, 0.0))
    per_channel = jnp.dot(
        spreads, group_matrix((128, CH), 0), precision=HIGH, preferred_element_type=F32
    )
    mean = per_channel[0:1]
    scale = per_channel[1:2] * gain1_ref[...]
    bias = bias1_ref[...]

    def activate(i):
        at = pl.ds(pl.multiple_of(i * 32, 32), 32)
        act[at] = silu((xg[at].astype(F32) - mean) * scale + bias).astype(BF16)

    loop(FRAMES * PLANE // 32, activate)

    to_next = (lax.rem(t + 1, 16), r)

    def convolve(weights, product, which, between):
        taps[...] = jnp.zeros_like(taps)

        def step(i, first):
            frame = first - i // 3
            tap_time = lax.rem(i, 3)
            rows = weights[pl.ds(pl.multiple_of(tap_time * TAPS, 16), TAPS)]
            taps[frame + 2 - tap_time] += product(rows, frame)

        loop(6, lambda i: step(i, 2))
        halo_out[which, 0] = combine(taps[3])
        halo_out[which, 1] = combine(taps[4])

        @pl.when(t < 15)
        def _():
            push(
                halo_out.at[which],
                halo_in.at[which],
                shalo_send.at[which],
                shalo.at[which],
                to_next,
            )

        loop(3, lambda i: step(i, 0))
        results = [combine(taps[frame]) for frame in range(FRAMES)]
        between()

        @pl.when(t > 0)
        def _():
            await_recv(halo_in.at[which], shalo.at[which])

        results[0] = results[0] + halo_in[which, 0]
        results[1] = results[1] + halo_in[which, 1]
        return results

    def product_one(rows, frame):
        at = pl.ds(pl.multiple_of(frame * PLANE, PLANE), PLANE)
        return lax.dot_general(rows, act[at], NT, preferred_element_type=F32)

    def product_two(rows, frame):
        at = pl.ds(pl.multiple_of(frame * CH, CH), CH)
        return jnp.dot(rows, hg[at], preferred_element_type=F32)

    load1.wait()
    hidden = [
        value.astype(BF16).astype(F32)
        for value in convolve(w1, product_one, 0, lambda: expand_step(1))
    ]

    added = hidden[0] + hidden[1] + hidden[2]
    squared = hidden[0] * hidden[0] + hidden[1] * hidden[1] + hidden[2] * hidden[2]
    lines = []
    for field in (added, squared):
        field = field[:, :128] + field[:, 128:]
        for group in range(2):
            lines.append(jnp.sum(field[group * 24 : group * 24 + 24], axis=0, keepdims=True))
    message = jnp.zeros((8, 128), F32)
    for i, line in enumerate(lines):
        message = jnp.where(row8 == i, line, message)
    stat_two[t] = message

    def exchange_two(i):
        push(
            stat_two.at[t],
            stat_two.at[t],
            sstat_send.at[2],
            sstat.at[2],
            (lax.rem(t + 1 + i, 16), r),
        )

    loop(15, exchange_two)
    pick = iota((OWN, CH), 1) == r * OWN + iota((OWN, CH), 0)
    gain = jnp.sum(jnp.where(pick, gain2_ref[...], 0.0), axis=1, keepdims=True)
    bias = jnp.sum(jnp.where(pick, bias2_ref[...], 0.0), axis=1, keepdims=True)
    await_recv(stat_two.at[pl.ds(0, 15)], sstat.at[2])
    averages = jnp.sum(jnp.sum(stat_two[...], axis=0), axis=1, keepdims=True) * (1.0 / COUNT)
    group = iota((OWN, 1), 0) < 24
    mean = jnp.where(group, averages[0:1], averages[1:2])
    square = jnp.where(group, averages[2:3], averages[3:4])
    scale = lax.rsqrt(square - mean * mean + 1e-06) * gain
    for frame in range(FRAMES):
        at = pl.ds(pl.multiple_of(frame * CH + r * OWN, 16), OWN)
        hg[at] = silu((hidden[frame] - mean) * scale + bias).astype(BF16)

    ring(view_h, sh_send, sh, lambda: expand_step(2))

    load2.wait()
    expand_step(3)
    sums = convolve(w2, product_two, 1, lambda: expand_step(4))
    pick = pick.astype(BF16)
    for frame in range(FRAMES):
        residual = lax.dot_general(
            pick, xg[frame * PLANE : (frame + 1) * PLANE], NT, preferred_element_type=F32
        )
        hid[frame] = (sums[frame] + residual).astype(BF16).astype(F32)

    lane = iota((OWN, 128), 1)
    for part in range(2):
        for line in range(8):
            total = jnp.zeros((OWN, 128), F32)
            for frame in range(FRAMES):
                moved = pltpu.roll(
                    hid[frame, :, part * 128 : part * 128 + 128], (16 * (frame - line)) % 128, 1
                )
                total = jnp.where(lane >> 4 == frame, moved, total)
            pack[part * 8 + line] = total.astype(BF16)
    mine = pl.ds(pl.multiple_of(r * OWN, 16), OWN)
    sg[mine] = pack[r]

    def to_rows(i):
        other = lax.rem(r + 1 + i, 16)
        push(pack.at[other], sg.at[mine], sg_send, sg_recv, (t, other))

    loop(15, to_rows)
    loop(8, expand_across)
    loop(15, expand_last)
    await_recv(sg.at[pl.ds(0, 15 * OWN)], sg_recv)

    lane = iota((128, 128), 1)
    source = ((lane >> 5) << 4) + ((lane & 31) >> 1)
    double = ((iota((128, 128), 0) == source) & (lane < 96)).astype(BF16)
    doubled = jnp.dot(sg[...], double, preferred_element_type=F32).astype(BF16)
    even = (iota((512, 128), 1) & 1) == 0

    def expand(i):
        one = jnp.dot(ekt[2 * i], doubled, preferred_element_type=F32)
        two = jnp.dot(ekt[2 * i + 1], doubled, preferred_element_type=F32)
        turned = jnp.where(even, one, two).T.astype(BF16)
        for frame in range(FRAMES):
            out_ref[3 * frame + i // 2, lax.rem(i, 2)] = turned[frame * 32 : frame * 32 + 32]

    loop(6, expand)

    await_recv(xg.at[pl.ds(0, 15 * 48)], sx_send)
    await_recv(hg.at[pl.ds(0, 15 * 144)], sh_send)
    for _ in range(2):
        await_recv(ekt.at[pl.ds(0, 6), pl.ds(0, 480)], se_send)
    await_recv(stat_rows.at[pl.ds(0, 15)], sstat_send.at[0])
    await_recv(stat_tm.at[pl.ds(0, 15)], sstat_send.at[1])
    await_recv(stat_two.at[pl.ds(0, 15)], sstat_send.at[2])
    await_recv(sg.at[pl.ds(0, 15 * OWN)], sg_send)

    @pl.when(t < 15)
    def _():
        await_recv(halo_out.at[0], shalo_send.at[0])
        await_recv(halo_out.at[1], shalo_send.at[1])


def shards(
    latents,
    first_gain,
    first_bias,
    second_gain,
    second_bias,
    first_kernel,
    second_kernel,
    expand_kernel,
):
    vmem = pl.BlockSpec(memory_space=pltpu.VMEM)
    anywhere = pl.BlockSpec(memory_space=pl.ANY)
    dma = pltpu.SemaphoreType.DMA
    return pl.pallas_call(
        kernel,
        out_shape=jax.ShapeDtypeStruct((9, 2, 32, 512), BF16),
        in_specs=[vmem] * 5 + [anywhere] * 2 + [vmem],
        out_specs=vmem,
        scratch_shapes=[
            pltpu.VMEM((27 * OWN, CH), BF16),
            pltpu.VMEM((27 * OWN, CH), BF16),
            pltpu.VMEM((FRAMES * PLANE, CH), BF16),
            pltpu.VMEM((FRAMES * PLANE, CH), BF16),
            pltpu.VMEM((FRAMES * CH, PLANE), BF16),
            pltpu.VMEM((12, 512, CH), BF16),
            pltpu.VMEM((5, TAPS, PLANE), F32),
            pltpu.VMEM((FRAMES, OWN, PLANE), F32),
            pltpu.VMEM((2, 2, OWN, PLANE), F32),
            pltpu.VMEM((2, 2, OWN, PLANE), F32),
            pltpu.VMEM((16, 8, 128), F32),
            pltpu.VMEM((16, 8, 128), F32),
            pltpu.VMEM((16, 8, 128), F32),
            pltpu.VMEM((16, OWN, 128), BF16),
            pltpu.VMEM((CH, 128), BF16),
            dma((2,)),
            dma,
            dma((16, FRAMES)),
            dma,
            dma((16, FRAMES)),
            dma,
            dma((2, 16)),
            dma((3,)),
            dma((3,)),
            dma((2,)),
            dma((2,)),
            dma,
            dma,
        ],
        compiler_params=pltpu.CompilerParams(
            collective_id=0, has_side_effects=True, vmem_limit_bytes=48 << 20
        ),
        name="block",
    )(
        latents.reshape(48, CH),
        first_gain.reshape(1, CH),
        first_bias.reshape(1, CH),
        second_gain.reshape(1, CH),
        second_bias.reshape(1, CH),
        first_kernel.reshape(27 * OWN, CH),
        second_kernel.reshape(27 * OWN, CH),
        expand_kernel,
    )


def solution(mesh):
    return jax.shard_map(
        shards,
        mesh=mesh,
        in_specs=(
            P("tm", "rows", None, None),
            P(),
            P(),
            P(),
            P(),
            P(None, None, None, "rows", None),
            P(None, None, None, "rows", None),
            P(None, "rows"),
        ),
        out_specs=P("tm", "rows", None, None),
        check_vma=False,
    )
```

```python
import jax
import jax.numpy as jnp
from jax import lax
from jax.experimental import pallas as pl
from jax.experimental.pallas import tpu as pltpu
from jax.sharding import PartitionSpec as P

MESH = pl.DeviceIdType.MESH
BF16 = jnp.bfloat16
F32 = jnp.float32
HIGH = lax.Precision.HIGHEST

CH = 768
OWN = 48
FRAMES = 3
PLANE = 256
TAPS = 9 * OWN
COUNT = 48 * 16 * 16 * 24
NT = (((1,), (1,)), ((), ()))


def iota(shape, axis):
    return lax.broadcasted_iota(jnp.int32, shape, axis)


def loop(count, body):
    def step(i, carry):
        body(i)
        return carry

    lax.fori_loop(0, count, step, 0)


def push(src, dst, send_sem, recv_sem, device):
    pltpu.make_async_remote_copy(
        src_ref=src,
        dst_ref=dst,
        send_sem=send_sem,
        recv_sem=recv_sem,
        device_id=device,
        device_id_type=MESH,
    ).start()


def await_recv(ref, sem):
    pltpu.make_async_copy(ref, ref, sem).wait()


def combine(taps):
    lane = iota((OWN, PLANE), 1)
    column = lane & 15
    total = None
    for tap_row in range(3):
        base = tap_row * 3 * OWN
        line = taps[base + OWN : base + 2 * OWN]
        line += jnp.where(column != 0, pltpu.roll(taps[base : base + OWN], 1, 1), 0.0)
        line += jnp.where(
            column != 15, pltpu.roll(taps[base + 2 * OWN : base + 3 * OWN], PLANE - 1, 1), 0.0
        )
        if tap_row == 0:
            line = jnp.where(lane >= 16, pltpu.roll(line, 16, 1), 0.0)
        elif tap_row == 2:
            line = jnp.where(lane < PLANE - 16, pltpu.roll(line, PLANE - 16, 1), 0.0)
        total = line if total is None else total + line
    return total


def silu(value):
    return value * jax.nn.sigmoid(value)


def group_matrix(shape, group_axis):
    channel = iota(shape, 1 - group_axis)
    return ((channel * 2731) >> 16 == iota(shape, group_axis)).astype(F32)


def kernel(
    x_hbm,
    gain1_ref,
    bias1_ref,
    gain2_ref,
    bias2_ref,
    w1_hbm,
    w2_hbm,
    ek_hbm,
    out_ref,
    x_ref,
    ek_ref,
    w1,
    w2,
    xg,
    act,
    hg,
    act_two,
    ekt,
    taps,
    results,
    hid,
    halo_out,
    halo_in,
    stat_rows,
    stat_tm,
    stat_two,
    norms,
    gain_columns,
    bias_columns,
    across,
    pack,
    sg,
    sem_w,
    sx_send,
    sx,
    sh_send,
    sh,
    se_send,
    se,
    sstat_send,
    sstat,
    shalo_send,
    shalo,
    sg_send,
    sg_recv,
    so_send,
    so_recv,
):
    t = lax.axis_index("tm")
    r = lax.axis_index("rows")
    xh = r // 8
    z = lax.rem(r, 8)
    half = lax.rem(t, 2)

    def slot(other, distance):
        line = 1 - xh if other else xh
        return line * 8 + lax.rem(z + distance + 8, 8)

    up = (t, slot(False, 1))
    down = (t, slot(False, -1))
    partner = (t, slot(True, 0))
    sibling = (t + 1 - 2 * half, r)

    load_x = pltpu.make_async_copy(x_hbm, x_ref, sem_w.at[0])
    load_e = pltpu.make_async_copy(ek_hbm, ek_ref, sem_w.at[1])
    load1 = pltpu.make_async_copy(w1_hbm, w1, sem_w.at[2])
    load2 = pltpu.make_async_copy(w2_hbm, w2, sem_w.at[3])
    for load in (load_x, load_e, load1, load2):
        load.start()

    barrier = pltpu.get_barrier_semaphore()

    def greet(i):
        pl.semaphore_signal(
            barrier, inc=1, device_id=(t, lax.rem(r + 1 + i, 16)), device_id_type=MESH
        )
        pl.semaphore_signal(
            barrier, inc=1, device_id=(lax.rem(t + 1 + i, 16), r), device_id_type=MESH
        )

    loop(15, greet)

    load_x.wait()
    for frame in range(FRAMES):
        xg[pl.ds(pl.multiple_of(frame * PLANE + r * 16, 16), 16)] = x_ref[
            frame * 16 : frame * 16 + 16
        ]
    own = x_ref[...].astype(F32)
    row8 = iota((8, CH), 0)
    sums = jnp.where(
        row8 == 0,
        jnp.sum(own, axis=0, keepdims=True),
        jnp.where(row8 == 1, jnp.sum(own * own, axis=0, keepdims=True), 0.0),
    )
    stat_rows[r] = jnp.dot(
        sums, group_matrix((CH, 128), 1), precision=HIGH, preferred_element_type=F32
    )

    @pl.when(t == 0)
    def _():
        halo_in[...] = jnp.zeros_like(halo_in)

    pl.semaphore_wait(barrier, 30)

    def exchange_rows(i):
        push(
            stat_rows.at[r],
            stat_rows.at[r],
            sstat_send.at[0],
            sstat.at[0],
            (t, lax.rem(r + 1 + i, 16)),
        )

    loop(15, exchange_rows)

    plan = [
        (False, 0, ("x", 2, -2, 1, -1)),
        (False, -2, (2, 1, "x")),
        (False, 2, (-1, "x")),
        (False, -1, ("x",)),
        (False, 1, ("x",)),
        (False, -3, ("x",)),
        (False, 3, ("x",)),
        (False, -4, ("x",)),
    ] + [(True, distance, ()) for distance in (0, -2, 2, -1, 1, -3, 3, -4)]

    def ring(view, send_sem, sems, hooks):
        for place, (other, distance, targets) in enumerate(plan):
            which = slot(other, distance)
            devices = [partner if to == "x" else (t, slot(False, to)) for to in targets]

            def piece(i, which=which, devices=devices, place=place):
                frame = FRAMES - 1 - i
                ref = view(which, frame)
                if place:
                    await_recv(ref, sems.at[which, frame])
                for device in devices:
                    push(ref, ref, send_sem, sems.at[which, frame], device)

            loop(FRAMES, piece)
            if place in hooks:
                hooks[place]()

    def view_x(which, frame):
        return xg.at[pl.ds(pl.multiple_of(frame * PLANE + which * 16, 16), 16)]

    def view_h(which, frame):
        return hg.at[pl.ds(pl.multiple_of(frame * CH + which * OWN, 16), OWN)]

    def exchange_tm():
        await_recv(stat_rows.at[pl.ds(0, 15)], sstat.at[0])
        stat_tm[t] = jnp.sum(stat_rows[...], axis=0)

        def send(i):
            push(
                stat_tm.at[t],
                stat_tm.at[t],
                sstat_send.at[1],
                sstat.at[1],
                (lax.rem(t + 1 + i, 16), r),
            )

        loop(15, send)

    def expand_prepare():
        load_e.wait()
        row = iota((384, 384), 0)
        place = (iota((384, 384), 1) == 12 * (row & 31) + (row >> 5)).astype(BF16)
        turned = lax.dot_general(place, ek_ref[...], NT, preferred_element_type=F32).astype(BF16)
        for sub in range(12):
            ekt[sub, pl.ds(pl.multiple_of(z * 32, 32), 32)] = turned[sub * 32 : sub * 32 + 32]
        expand_start()

    def view_e(part, which):
        return ekt.at[pl.ds(part * 6, 6), pl.ds(pl.multiple_of(which * 32, 32), 32)]

    def send_e(which, device):
        ref = view_e(half, which)
        push(ref, ref, se_send, se.at[half, which], device)

    def expand_start():
        send_e(z, up)
        send_e(z, down)

    def expand_step(step):
        for sign, last in ((-1, 4), (1, 3)):
            if step > last:
                continue
            which = lax.rem(z + sign * step + 8, 8)
            await_recv(view_e(half, which), se.at[half, which])
            if step < last:
                send_e(which, up if sign == -1 else down)
            send_e(which, sibling)

    def expand_last(i):
        which = lax.rem(z + 1 + i, 8)
        await_recv(view_e(1 - half, which), se.at[1 - half, which])

    ring(view_x, sx_send, sx, {0: expand_prepare, 7: exchange_tm})
    expand_step(1)

    await_recv(stat_tm.at[pl.ds(0, 15)], sstat.at[1])
    averages = jnp.sum(stat_tm[...], axis=0) * (1.0 / COUNT)
    mean, square = averages[0:1], averages[1:2]
    inverse = lax.rsqrt(square - mean * mean + 1e-06)
    row8 = iota((8, 128), 0)
    spreads = jnp.where(row8 == 0, mean, jnp.where(row8 == 1, inverse, 0.0))
    per_channel = jnp.dot(
        spreads, group_matrix((128, CH), 0), precision=HIGH, preferred_element_type=F32
    )
    mean = per_channel[0:1]
    scale = per_channel[1:2] * gain1_ref[...].reshape(1, CH)
    bias = bias1_ref[...].reshape(1, CH)

    def activate(i):
        at = pl.ds(pl.multiple_of(i * 32, 32), 32)
        act[at] = silu((xg[at].astype(F32) - mean) * scale + bias).astype(BF16)

    loop(FRAMES * PLANE // 32, activate)

    to_next = (lax.rem(t + 1, 16), r)

    def convolve(weights, product, which, between):
        def result(i):
            out_frame = 4 - i
            first = jnp.maximum(out_frame - 2, 0)
            taps[...] = jnp.zeros_like(taps)

            def step(frame, carry):
                tap_time = frame + 2 - out_frame
                rows = weights[pl.ds(pl.multiple_of(tap_time * TAPS, 16), TAPS)]
                taps[...] += product(rows, frame)
                return carry

            lax.fori_loop(first, jnp.minimum(out_frame, 2) + 1, step, 0)
            return combine(taps)

        def ahead(i):
            place = 1 - i
            halo_out[which, place] = result(i)

            @pl.when(t < 15)
            def _():
                push(
                    halo_out.at[which, place],
                    halo_in.at[which, place],
                    shalo_send.at[which],
                    shalo.at[which],
                    to_next,
                )

        def own(i):
            results[2 - i] = result(i + 2)

        loop(2, ahead)
        between()
        loop(3, own)

        @pl.when(t > 0)
        def _():
            await_recv(halo_in.at[which], shalo.at[which])

        return [
            results[0] + halo_in[which, 0],
            results[1] + halo_in[which, 1],
            results[2],
        ]

    def product_one(rows, frame):
        at = pl.ds(pl.multiple_of(frame * PLANE, PLANE), PLANE)
        return lax.dot_general(rows, act[at], NT, preferred_element_type=F32)

    def product_two(rows, frame):
        at = pl.ds(pl.multiple_of(frame * CH, CH), CH)
        return jnp.dot(rows, act_two[at], preferred_element_type=F32)

    load1.wait()
    hidden = [
        value.astype(BF16) for value in convolve(w1, product_one, 0, lambda: None)
    ]
    for frame in range(FRAMES):
        hg[pl.ds(pl.multiple_of(frame * CH + r * OWN, 16), OWN)] = hidden[frame]
    hidden = [value.astype(F32) for value in hidden]

    added = hidden[0] + hidden[1] + hidden[2]
    squared = hidden[0] * hidden[0] + hidden[1] * hidden[1] + hidden[2] * hidden[2]
    lines = []
    for field in (added, squared):
        field = field[:, :128] + field[:, 128:]
        for group in range(2):
            lines.append(jnp.sum(field[group * 24 : group * 24 + 24], axis=0, keepdims=True))
    message = jnp.zeros((8, 128), F32)
    for i, line in enumerate(lines):
        message = jnp.where(row8 == i, line, message)
    stat_two[t] = message

    def exchange_two(i):
        push(
            stat_two.at[t],
            stat_two.at[t],
            sstat_send.at[2],
            sstat.at[2],
            (lax.rem(t + 1 + i, 16), r),
        )

    def residuals():
        loop(15, exchange_two)
        pick = (iota((OWN, CH), 1) == r * OWN + iota((OWN, CH), 0)).astype(BF16)
        for frame in range(FRAMES):
            hid[frame] = lax.dot_general(
                pick, xg[frame * PLANE : (frame + 1) * PLANE], NT, preferred_element_type=F32
            )
        gain_columns[...] = jnp.broadcast_to(gain2_ref[...].reshape(1, CH), (128, CH)).T
        bias_columns[...] = jnp.broadcast_to(bias2_ref[...].reshape(1, CH), (128, CH)).T

    def spread_two():
        await_recv(stat_two.at[pl.ds(0, 15)], sstat.at[2])
        averages = jnp.sum(jnp.sum(stat_two[...], axis=0), axis=1, keepdims=True) * (1.0 / COUNT)
        averages = jnp.broadcast_to(averages, (8, 128))
        mean = averages[0:2]
        inverse = lax.rsqrt(averages[2:4] - mean * mean + 1e-06)
        norms[r] = jnp.where(
            row8 == 0,
            mean[0:1],
            jnp.where(row8 == 1, mean[1:2], jnp.where(row8 == 2, inverse[0:1], inverse[1:2])),
        )

        def send(i):
            push(
                norms.at[r],
                norms.at[r],
                sstat_send.at[3],
                sstat.at[3],
                (t, lax.rem(r + 1 + i, 16)),
            )

        loop(15, send)

    def after_line():
        spread_two()
        expand_step(2)

    ring(view_h, sh_send, sh, {0: residuals, 7: after_line})
    await_recv(norms.at[pl.ds(0, 15)], sstat.at[3])
    lower = iota((OWN, 128), 0) < 24

    def activate_two(i):
        source = lax.rem(i, 16)
        at = pl.ds(pl.multiple_of(i * OWN, 16), OWN)
        channels = pl.ds(pl.multiple_of(source * OWN, 16), OWN)
        norm = norms[source]
        mean = jnp.where(lower, norm[0:1], norm[1:2])
        scale = jnp.where(lower, norm[2:3], norm[3:4]) * gain_columns[channels]
        bias = bias_columns[channels]
        value = hg[at].astype(F32)
        act_two[at] = jnp.concatenate(
            [
                silu((value[:, part * 128 : part * 128 + 128] - mean) * scale + bias)
                for part in range(2)
            ],
            axis=1,
        ).astype(BF16)

    load2.wait()
    loop(16 * FRAMES, activate_two)
    sums = convolve(w2, product_two, 1, lambda: expand_step(3))
    for frame in range(FRAMES):
        hid[frame] = (sums[frame] + hid[frame]).astype(BF16).astype(F32)

    lane = iota((OWN, 128), 1)
    for line in range(8):
        total = jnp.zeros((OWN, 128), F32)
        for part in range(2):
            for frame in range(FRAMES):
                place = 3 * part + frame
                moved = pltpu.roll(
                    hid[frame, :, part * 128 : part * 128 + 128], (16 * (place - line)) % 128, 1
                )
                total = jnp.where(lane >> 4 == place, moved, total)
        pack[line] = total.astype(BF16)
    mine = pl.ds(pl.multiple_of(r * OWN, 16), OWN)
    sg[mine] = pack[z]

    def to_rows(i):
        other = lax.rem(r + 1 + i, 16)
        push(pack.at[lax.rem(other, 8)], sg.at[mine], sg_send, sg_recv, (t, other))

    loop(15, to_rows)
    expand_step(4)
    loop(7, expand_last)
    column = iota((128, PLANE), 1)
    second = (column >= 96).astype(jnp.int32)
    inside = column - 96 * second
    source = 48 * (second + xh - 2 * xh * second) + ((inside >> 5) << 4) + ((inside & 31) >> 1)
    double = ((iota((128, PLANE), 0) == source) & (column < 192)).astype(BF16)
    even = (iota((PLANE, PLANE), 1) & 1) == 0
    await_recv(sg.at[pl.ds(0, 15 * OWN)], sg_recv)

    doubled = jnp.dot(sg[...], double, preferred_element_type=F32).astype(BF16)
    own_half = pl.ds(pl.multiple_of(xh * 256, 256), 256)
    other_half = pl.ds(pl.multiple_of(256 - xh * 256, 256), 256)

    def expand(i):
        one = jnp.dot(ekt[2 * i], doubled, preferred_element_type=F32)
        two = jnp.dot(ekt[2 * i + 1], doubled, preferred_element_type=F32)
        turned = jnp.where(even, one, two).T.astype(BF16)
        tap_time, tap_row = i // 2, lax.rem(i, 2)
        for frame in range(FRAMES):
            out_ref[frame, tap_time, tap_row, :, own_half] = turned[frame * 32 : frame * 32 + 32]
            across[i, frame] = turned[96 + frame * 32 : 128 + frame * 32]
        push(
            across.at[i],
            out_ref.at[:, tap_time, tap_row, :, own_half],
            so_send,
            so_recv,
            partner,
        )

    loop(6, expand)
    await_recv(out_ref.at[:, :, :, :, other_half], so_recv)

    await_recv(xg.at[pl.ds(0, 15 * 48)], sx_send)
    await_recv(hg.at[pl.ds(0, 15 * 144)], sh_send)
    for _ in range(2):
        await_recv(ekt.at[pl.ds(0, 6), pl.ds(0, 224)], se_send)
    await_recv(norms.at[pl.ds(0, 15)], sstat_send.at[3])
    await_recv(across, so_send)
    await_recv(stat_rows.at[pl.ds(0, 15)], sstat_send.at[0])
    await_recv(stat_tm.at[pl.ds(0, 15)], sstat_send.at[1])
    await_recv(stat_two.at[pl.ds(0, 15)], sstat_send.at[2])
    await_recv(sg.at[pl.ds(0, 15 * OWN)], sg_send)

    @pl.when(t < 15)
    def _():
        await_recv(halo_out.at[0], shalo_send.at[0])
        await_recv(halo_out.at[1], shalo_send.at[1])


def shards(
    latents,
    first_gain,
    first_bias,
    second_gain,
    second_bias,
    first_kernel,
    second_kernel,
    expand_kernel,
):
    vmem = pl.BlockSpec(memory_space=pltpu.VMEM)
    anywhere = pl.BlockSpec(memory_space=pl.ANY)
    dma = pltpu.SemaphoreType.DMA
    return pl.pallas_call(
        kernel,
        out_shape=jax.ShapeDtypeStruct((FRAMES, 3, 2, 32, 512), BF16),
        in_specs=[anywhere] + [vmem] * 4 + [anywhere] * 3,
        out_specs=vmem,
        scratch_shapes=[
            pltpu.VMEM((48, CH), BF16),
            pltpu.VMEM((CH, 384), BF16),
            pltpu.VMEM((27 * OWN, CH), BF16),
            pltpu.VMEM((27 * OWN, CH), BF16),
            pltpu.VMEM((FRAMES * PLANE, CH), BF16),
            pltpu.VMEM((FRAMES * PLANE, CH), BF16),
            pltpu.VMEM((FRAMES * CH, PLANE), BF16),
            pltpu.VMEM((FRAMES * CH, PLANE), BF16),
            pltpu.VMEM((12, 256, CH), BF16),
            pltpu.VMEM((TAPS, PLANE), F32),
            pltpu.VMEM((FRAMES, OWN, PLANE), F32),
            pltpu.VMEM((FRAMES, OWN, PLANE), F32),
            pltpu.VMEM((2, 2, OWN, PLANE), F32),
            pltpu.VMEM((2, 2, OWN, PLANE), F32),
            pltpu.VMEM((16, 8, 128), F32),
            pltpu.VMEM((16, 8, 128), F32),
            pltpu.VMEM((16, 8, 128), F32),
            pltpu.VMEM((16, 8, 128), F32),
            pltpu.VMEM((CH, 128), F32),
            pltpu.VMEM((CH, 128), F32),
            pltpu.VMEM((6, FRAMES, 32, 256), BF16),
            pltpu.VMEM((8, OWN, 128), BF16),
            pltpu.VMEM((CH, 128), BF16),
            dma((4,)),
            dma,
            dma((16, FRAMES)),
            dma,
            dma((16, FRAMES)),
            dma,
            dma((2, 8)),
            dma((4,)),
            dma((4,)),
            dma((2,)),
            dma((2,)),
            dma,
            dma,
            dma,
            dma,
        ],
        compiler_params=pltpu.CompilerParams(
            collective_id=0, has_side_effects=True, vmem_limit_bytes=60 << 20
        ),
        name="block",
    )(
        latents.reshape(48, CH),
        first_gain,
        first_bias,
        second_gain,
        second_bias,
        first_kernel.reshape(27 * OWN, CH),
        second_kernel.reshape(27 * OWN, CH),
        expand_kernel,
    ).reshape(3 * FRAMES, 2, 32, 512)


def solution(mesh):
    return jax.shard_map(
        shards,
        mesh=mesh,
        in_specs=(
            P("tm", "rows", None, None),
            P(),
            P(),
            P(),
            P(),
            P(None, None, None, "rows", None),
            P(None, None, None, "rows", None),
            P(None, "rows"),
        ),
        out_specs=P("tm", "rows", None, None),
        check_vma=False,
    )
```

```python
import jax
import jax.numpy as jnp
from jax import lax
from jax.experimental import pallas as pl
from jax.experimental.pallas import tpu as pltpu
from jax.sharding import PartitionSpec as P

MESH = pl.DeviceIdType.MESH
BF16 = jnp.bfloat16
F32 = jnp.float32
HIGH = lax.Precision.HIGHEST

CH = 768
OWN = 48
FRAMES = 3
PLANE = 256
TAPS = 9 * OWN
COUNT = 48 * 16 * 16 * 24
NT = (((1,), (1,)), ((), ()))


def iota(shape, axis):
    return lax.broadcasted_iota(jnp.int32, shape, axis)


def loop(count, body):
    def step(i, carry):
        body(i)
        return carry

    lax.fori_loop(0, count, step, 0)


def push(src, dst, send_sem, recv_sem, device):
    pltpu.make_async_remote_copy(
        src_ref=src,
        dst_ref=dst,
        send_sem=send_sem,
        recv_sem=recv_sem,
        device_id=device,
        device_id_type=MESH,
    ).start()


def await_recv(ref, sem):
    pltpu.make_async_copy(ref, ref, sem).wait()


def combine(taps):
    lane = iota((OWN, PLANE), 1)
    column = lane & 15
    total = None
    for tap_row in range(3):
        base = tap_row * 3 * OWN
        line = taps[base + OWN : base + 2 * OWN]
        line += jnp.where(column != 0, pltpu.roll(taps[base : base + OWN], 1, 1), 0.0)
        line += jnp.where(
            column != 15, pltpu.roll(taps[base + 2 * OWN : base + 3 * OWN], PLANE - 1, 1), 0.0
        )
        if tap_row == 0:
            line = jnp.where(lane >= 16, pltpu.roll(line, 16, 1), 0.0)
        elif tap_row == 2:
            line = jnp.where(lane < PLANE - 16, pltpu.roll(line, PLANE - 16, 1), 0.0)
        total = line if total is None else total + line
    return total


def silu(value):
    return value * jax.nn.sigmoid(value)


def group_matrix(shape, group_axis):
    channel = iota(shape, 1 - group_axis)
    return ((channel * 2731) >> 16 == iota(shape, group_axis)).astype(F32)


def kernel(
    x_hbm,
    gain1_hbm,
    bias1_hbm,
    gain2_hbm,
    bias2_hbm,
    w1_hbm,
    w2_hbm,
    ek_hbm,
    out_ref,
    gain1_ref,
    bias1_ref,
    gain2_ref,
    bias2_ref,
    x_ref,
    ek_ref,
    w1,
    w2,
    xg,
    act,
    hg,
    act_two,
    ekt,
    taps,
    results,
    hid,
    halo_out,
    halo_in,
    stat_rows,
    stat_tm,
    stat_two,
    norms,
    gain_columns,
    bias_columns,
    across,
    pack,
    sg,
    sem_w,
    sx_send,
    sx,
    sh_send,
    sh,
    se_send,
    se,
    sstat_send,
    sstat,
    shalo_send,
    shalo,
    sg_send,
    sg_recv,
    so_send,
    so_recv,
):
    t = lax.axis_index("tm")
    r = lax.axis_index("rows")
    xh = r // 8
    z = lax.rem(r, 8)
    half = lax.rem(t, 2)

    def slot(other, distance):
        line = 1 - xh if other else xh
        return line * 8 + lax.rem(z + distance + 8, 8)


    partner = (t, slot(True, 0))
    sibling = (t + 1 - 2 * half, r)

    lines = ((True, 4), (True, 3), (True, -3), (False, 4), (True, 2), (True, -2), (False, 3), (False, -3))
    lines += ((True, 1), (True, -1), (True, 0), (False, 2), (False, -2), (False, 1), (False, -1))
    row_peers = [slot(other, distance) for other, distance in lines]
    block, plane = t // 8, lax.rem(t, 8) // 2
    steps = ((1, 2), (0, 2), (1, 1), (1, 3), (0, 1), (0, 3), (1, 0))
    tm_peers = [
        lax.rem(block + across_x, 2) * 8 + lax.rem(plane + up_y, 4) * 2 + core
        for across_x, up_y in steps
        for core in range(2)
    ] + [t + 1 - 2 * half]

    load_x = pltpu.make_async_copy(x_hbm, x_ref, sem_w.at[0])
    load_e = pltpu.make_async_copy(ek_hbm, ek_ref, sem_w.at[1])
    load1 = pltpu.make_async_copy(w1_hbm, w1, sem_w.at[2])
    load2 = pltpu.make_async_copy(w2_hbm, w2, sem_w.at[3])
    load_small = [
        pltpu.make_async_copy(src, dst, sem_w.at[4 + i])
        for i, (src, dst) in enumerate(
            (
                (gain1_hbm, gain1_ref),
                (bias1_hbm, bias1_ref),
                (gain2_hbm, gain2_ref),
                (bias2_hbm, bias2_ref),
            )
        )
    ]
    for load in [load_x, load_e, load1, load2] + load_small:
        load.start()

    barrier = pltpu.get_barrier_semaphore()

    for peer in row_peers:
        pl.semaphore_signal(barrier, inc=1, device_id=(t, peer), device_id_type=MESH)
    for peer in tm_peers:
        pl.semaphore_signal(barrier, inc=1, device_id=(peer, r), device_id_type=MESH)

    load_x.wait()
    for load in load_small:
        load.wait()
    for frame in range(FRAMES):
        xg[frame, pl.ds(pl.multiple_of(r * 16, 16), 16)] = x_ref[
            frame * 16 : frame * 16 + 16
        ]
    own = x_ref[...].astype(F32)
    row8 = iota((8, CH), 0)
    sums = jnp.where(
        row8 == 0,
        jnp.sum(own, axis=0, keepdims=True),
        jnp.where(row8 == 1, jnp.sum(own * own, axis=0, keepdims=True), 0.0),
    )
    stat_rows[r] = jnp.dot(
        sums, group_matrix((CH, 128), 1), precision=HIGH, preferred_element_type=F32
    )

    @pl.when(t == 0)
    def _():
        halo_in[...] = jnp.zeros_like(halo_in)

    pl.semaphore_wait(barrier, 30)

    def tell_rows(ref, place):
        for peer in row_peers:
            push(ref, ref, sstat_send.at[place], sstat.at[place], (t, peer))

    def tell_tm(ref, place):
        for peer in tm_peers:
            push(ref, ref, sstat_send.at[place], sstat.at[place], (peer, r))

    tell_rows(stat_rows.at[r], 0)

    plan = [
        (False, 0, ("x", 2, -2, 1, -1)),
        (False, -2, (2, 1, "x")),
        (False, 2, (-1, "x")),
        (False, -1, ("x",)),
        (False, 1, ("x",)),
        (False, -3, ("x",)),
        (False, 3, ("x",)),
        (False, -4, ("x",)),
    ] + [(True, distance, ()) for distance in (0, -2, 2, -1, 1, -3, 3, -4)]

    def ring(view, send_sem, sems, hooks):
        for place, (other, distance, targets) in enumerate(plan):
            which = slot(other, distance)
            devices = [partner if to == "x" else (t, slot(False, to)) for to in targets]

            def piece(i, which=which, devices=devices, place=place):
                frame = FRAMES - 1 - i
                ref = view(which, pl.ds(frame, 1))
                if place:
                    await_recv(ref, sems.at[which, frame])
                for device in devices:
                    push(ref, ref, send_sem, sems.at[which, frame], device)

            loop(FRAMES, piece)
            if place in hooks:
                hooks[place]()

    def view_x(which, frames):
        return xg.at[frames, pl.ds(pl.multiple_of(which * 16, 16), 16)]

    def view_h(which, frames):
        return hg.at[frames, pl.ds(pl.multiple_of(which * OWN, 16), OWN)]

    def exchange_tm():
        await_recv(stat_rows.at[pl.ds(0, 15)], sstat.at[0])
        stat_tm[t] = jnp.sum(stat_rows[...], axis=0)

        tell_tm(stat_tm.at[t], 1)

    def expand_prepare():
        load_e.wait()
        row = iota((384, 384), 0)
        place = (iota((384, 384), 1) == 12 * (row & 31) + (row >> 5)).astype(BF16)
        turned = lax.dot_general(place, ek_ref[...], NT, preferred_element_type=F32).astype(BF16)
        for sub in range(12):
            ekt[sub, pl.ds(pl.multiple_of(z * 32, 32), 32)] = turned[sub * 32 : sub * 32 + 32]

    def view_e(part, which):
        return ekt.at[pl.ds(part * 6, 6), pl.ds(pl.multiple_of(which * 32, 32), 32)]

    def send_e(which, device):
        ref = view_e(half, which)
        push(ref, ref, se_send, se.at[half, which], device)

    up = (t, slot(False, 1))
    down = (t, slot(False, -1))
    def expand_start():
        send_e(z, up)
        send_e(z, down)

    def expand_step(step):
        for sign, last in ((-1, 4), (1, 3)):
            if step > last:
                continue
            which = lax.rem(z + sign * step + 8, 8)
            await_recv(view_e(half, which), se.at[half, which])
            if step < last:
                send_e(which, up if sign == -1 else down)
            send_e(which, sibling)

    def expand_last(i):
        which = lax.rem(z + 1 + i, 8)
        await_recv(view_e(1 - half, which), se.at[1 - half, which])

    ring(view_x, sx_send, sx, {0: expand_prepare, 5: exchange_tm, 7: expand_start})
    expand_step(1)
    await_recv(stat_tm.at[pl.ds(0, 15)], sstat.at[1])
    averages = jnp.sum(stat_tm[...], axis=0) * (1.0 / COUNT)
    mean, square = averages[0:1], averages[1:2]
    inverse = lax.rsqrt(square - mean * mean + 1e-06)
    row8 = iota((8, 128), 0)
    spreads = jnp.where(row8 == 0, mean, jnp.where(row8 == 1, inverse, 0.0))
    per_channel = jnp.dot(
        spreads, group_matrix((128, CH), 0), precision=HIGH, preferred_element_type=F32
    )
    mean = per_channel[0:1]
    scale = per_channel[1:2] * gain1_ref[...].reshape(1, CH)
    bias = bias1_ref[...].reshape(1, CH)

    def activate(i):
        at = pl.ds(pl.multiple_of(i * 32, 32), 32)
        part = pl.ds(pl.multiple_of(lax.rem(i, 8) * 32, 32), 32)
        act[at] = silu((xg[i // 8, part].astype(F32) - mean) * scale + bias).astype(BF16)

    loop(FRAMES * PLANE // 32, activate)

    to_next = (lax.rem(t + 1, 16), r)

    def convolve(weights, product, which, between):
        def result(i):
            out_frame = 4 - i
            first = jnp.maximum(out_frame - 2, 0)
            taps[...] = jnp.zeros_like(taps)

            def step(frame, carry):
                tap_time = frame + 2 - out_frame
                rows = weights[pl.ds(pl.multiple_of(tap_time * TAPS, 16), TAPS)]
                taps[...] += product(rows, frame)
                return carry

            lax.fori_loop(first, jnp.minimum(out_frame, 2) + 1, step, 0)
            return combine(taps)

        def ahead(i):
            place = 1 - i
            halo_out[which, place] = result(i)

            @pl.when(t < 15)
            def _():
                push(
                    halo_out.at[which, place],
                    halo_in.at[which, place],
                    shalo_send.at[which],
                    shalo.at[which],
                    to_next,
                )

        def own(i):
            results[2 - i] = result(i + 2)

        loop(2, ahead)
        between()
        loop(3, own)

        @pl.when(t > 0)
        def _():
            await_recv(halo_in.at[which], shalo.at[which])

        return [
            results[0] + halo_in[which, 0],
            results[1] + halo_in[which, 1],
            results[2],
        ]

    def product_one(rows, frame):
        at = pl.ds(pl.multiple_of(frame * PLANE, PLANE), PLANE)
        return lax.dot_general(rows, act[at], NT, preferred_element_type=F32)

    def product_two(rows, frame):
        at = pl.ds(pl.multiple_of(frame * CH, CH), CH)
        return jnp.dot(rows, act_two[at], preferred_element_type=F32)

    load1.wait()
    hidden = [
        value.astype(BF16) for value in convolve(w1, product_one, 0, lambda: None)
    ]
    for frame in range(FRAMES):
        hg[frame, pl.ds(pl.multiple_of(r * OWN, 16), OWN)] = hidden[frame]
    hidden = [value.astype(F32) for value in hidden]

    added = hidden[0] + hidden[1] + hidden[2]
    squared = hidden[0] * hidden[0] + hidden[1] * hidden[1] + hidden[2] * hidden[2]
    lines = []
    for field in (added, squared):
        field = field[:, :128] + field[:, 128:]
        for group in range(2):
            lines.append(jnp.sum(field[group * 24 : group * 24 + 24], axis=0, keepdims=True))
    message = jnp.zeros((8, 128), F32)
    for i, line in enumerate(lines):
        message = jnp.where(row8 == i, line, message)
    stat_two[t] = message

    def residuals():
        tell_tm(stat_two.at[t], 2)
        pick = (iota((OWN, CH), 1) == r * OWN + iota((OWN, CH), 0)).astype(BF16)
        for frame in range(FRAMES):
            hid[frame] = lax.dot_general(
                pick, xg[frame], NT, preferred_element_type=F32
            )
        gain_columns[...] = jnp.broadcast_to(gain2_ref[...].reshape(1, CH), (128, CH)).T
        bias_columns[...] = jnp.broadcast_to(bias2_ref[...].reshape(1, CH), (128, CH)).T

    def spread_two():
        await_recv(stat_two.at[pl.ds(0, 15)], sstat.at[2])
        averages = jnp.sum(jnp.sum(stat_two[...], axis=0), axis=1, keepdims=True) * (1.0 / COUNT)
        averages = jnp.broadcast_to(averages, (8, 128))
        mean = averages[0:2]
        inverse = lax.rsqrt(averages[2:4] - mean * mean + 1e-06)
        norms[r] = jnp.where(
            row8 == 0,
            mean[0:1],
            jnp.where(row8 == 1, mean[1:2], jnp.where(row8 == 2, inverse[0:1], inverse[1:2])),
        )

        tell_rows(norms.at[r], 3)

    def after_line():
        spread_two()
        expand_step(2)

    ring(view_h, sh_send, sh, {0: residuals, 7: after_line})
    await_recv(norms.at[pl.ds(0, 15)], sstat.at[3])
    lower = iota((OWN, 128), 0) < 24

    def activate_two(i):
        source = lax.rem(i, 16)
        at = pl.ds(pl.multiple_of(i * OWN, 16), OWN)
        channels = pl.ds(pl.multiple_of(source * OWN, 16), OWN)
        norm = norms[source]
        mean = jnp.where(lower, norm[0:1], norm[1:2])
        scale = jnp.where(lower, norm[2:3], norm[3:4]) * gain_columns[channels]
        bias = bias_columns[channels]
        value = hg[i // 16, channels].astype(F32)
        act_two[at] = jnp.concatenate(
            [
                silu((value[:, part * 128 : part * 128 + 128] - mean) * scale + bias)
                for part in range(2)
            ],
            axis=1,
        ).astype(BF16)

    load2.wait()
    loop(16 * FRAMES, activate_two)
    sums = convolve(w2, product_two, 1, lambda: expand_step(3))
    for frame in range(FRAMES):
        hid[frame] = (sums[frame] + hid[frame]).astype(BF16).astype(F32)

    lane = iota((OWN, 128), 1)
    for line in range(8):
        total = jnp.zeros((OWN, 128), F32)
        for part in range(2):
            for frame in range(FRAMES):
                place = 3 * part + frame
                moved = pltpu.roll(
                    hid[frame, :, part * 128 : part * 128 + 128], (16 * (place - line)) % 128, 1
                )
                total = jnp.where(lane >> 4 == place, moved, total)
        pack[line] = total.astype(BF16)
    mine = pl.ds(pl.multiple_of(r * OWN, 16), OWN)
    sg[mine] = pack[z]

    for peer in row_peers:
        push(pack.at[lax.rem(peer, 8)], sg.at[mine], sg_send, sg_recv, (t, peer))
    expand_step(4)
    loop(7, expand_last)
    column = iota((128, 128), 1)
    inside = ((column >> 5) << 4) + ((column & 31) >> 1)

    def double(line):
        return ((iota((128, 128), 0) == 48 * line + inside) & (column < 96)).astype(BF16)

    doubles = [double(1 - xh), double(xh)]
    even = (iota((256, 128), 1) & 1) == 0
    own_half = pl.ds(pl.multiple_of(xh * 256, 256), 256)
    other_half = pl.ds(pl.multiple_of(256 - xh * 256, 256), 256)
    await_recv(sg.at[pl.ds(0, 15 * OWN)], sg_recv)

    spread = [
        jnp.dot(sg[...], matrix, preferred_element_type=F32).astype(BF16) for matrix in doubles
    ]

    def rows_of(i, positions):
        both = jnp.dot(
            ekt[pl.ds(2 * i, 2)].reshape(512, CH), positions, preferred_element_type=F32
        )
        return jnp.where(even, both[:256], both[256:]).T.astype(BF16)

    def expand_other(i):
        turned = rows_of(i, spread[0])
        for frame in range(FRAMES):
            across[i, frame] = turned[frame * 32 : frame * 32 + 32]
        push(
            across.at[i],
            out_ref.at[:, i // 2, lax.rem(i, 2), :, own_half],
            so_send,
            so_recv,
            partner,
        )

    def expand_own(i):
        turned = rows_of(i, spread[1])
        for frame in range(FRAMES):
            out_ref[frame, i // 2, lax.rem(i, 2), :, own_half] = turned[
                frame * 32 : frame * 32 + 32
            ]

    loop(6, expand_other)
    loop(6, expand_own)
    await_recv(out_ref.at[:, :, :, :, other_half], so_recv)

    await_recv(xg.at[:, pl.ds(0, 15 * 16)], sx_send)
    await_recv(hg.at[:, pl.ds(0, 15 * OWN)], sh_send)
    for _ in range(2):
        await_recv(ekt.at[pl.ds(0, 6), pl.ds(0, 224)], se_send)
    await_recv(norms.at[pl.ds(0, 15)], sstat_send.at[3])
    await_recv(across, so_send)
    await_recv(stat_rows.at[pl.ds(0, 15)], sstat_send.at[0])
    await_recv(stat_tm.at[pl.ds(0, 15)], sstat_send.at[1])
    await_recv(stat_two.at[pl.ds(0, 15)], sstat_send.at[2])
    await_recv(sg.at[pl.ds(0, 15 * OWN)], sg_send)

    @pl.when(t < 15)
    def _():
        await_recv(halo_out.at[0], shalo_send.at[0])
        await_recv(halo_out.at[1], shalo_send.at[1])


def shards(
    latents,
    first_gain,
    first_bias,
    second_gain,
    second_bias,
    first_kernel,
    second_kernel,
    expand_kernel,
):
    vmem = pl.BlockSpec(memory_space=pltpu.VMEM)
    anywhere = pl.BlockSpec(memory_space=pl.ANY)
    dma = pltpu.SemaphoreType.DMA
    return pl.pallas_call(
        kernel,
        out_shape=jax.ShapeDtypeStruct((FRAMES, 3, 2, 32, 512), BF16),
        in_specs=[anywhere] * 8,
        out_specs=vmem,
        scratch_shapes=[pltpu.VMEM((CH,), F32)] * 4
        + [
            pltpu.VMEM((48, CH), BF16),
            pltpu.VMEM((CH, 384), BF16),
            pltpu.VMEM((27 * OWN, CH), BF16),
            pltpu.VMEM((27 * OWN, CH), BF16),
            pltpu.VMEM((FRAMES, PLANE, CH), BF16),
            pltpu.VMEM((FRAMES * PLANE, CH), BF16),
            pltpu.VMEM((FRAMES, CH, PLANE), BF16),
            pltpu.VMEM((FRAMES * CH, PLANE), BF16),
            pltpu.VMEM((12, 256, CH), BF16),
            pltpu.VMEM((TAPS, PLANE), F32),
            pltpu.VMEM((FRAMES, OWN, PLANE), F32),
            pltpu.VMEM((FRAMES, OWN, PLANE), F32),
            pltpu.VMEM((2, 2, OWN, PLANE), F32),
            pltpu.VMEM((2, 2, OWN, PLANE), F32),
            pltpu.VMEM((16, 8, 128), F32),
            pltpu.VMEM((16, 8, 128), F32),
            pltpu.VMEM((16, 8, 128), F32),
            pltpu.VMEM((16, 8, 128), F32),
            pltpu.VMEM((CH, 128), F32),
            pltpu.VMEM((CH, 128), F32),
            pltpu.VMEM((6, FRAMES, 32, 256), BF16),
            pltpu.VMEM((8, OWN, 128), BF16),
            pltpu.VMEM((CH, 128), BF16),
            dma((8,)),
            dma,
            dma((16, FRAMES)),
            dma,
            dma((16, FRAMES)),
            dma,
            dma((2, 8)),
            dma((4,)),
            dma((4,)),
            dma((2,)),
            dma((2,)),
            dma,
            dma,
            dma,
            dma,
        ],
        compiler_params=pltpu.CompilerParams(
            collective_id=0, has_side_effects=True, vmem_limit_bytes=60 << 20
        ),
        name="block",
    )(
        latents.reshape(48, CH),
        first_gain,
        first_bias,
        second_gain,
        second_bias,
        first_kernel.reshape(27 * OWN, CH),
        second_kernel.reshape(27 * OWN, CH),
        expand_kernel,
    ).reshape(3 * FRAMES, 2, 32, 512)


def solution(mesh):
    return jax.shard_map(
        shards,
        mesh=mesh,
        in_specs=(
            P("tm", "rows", None, None),
            P(),
            P(),
            P(),
            P(),
            P(None, None, None, "rows", None),
            P(None, None, None, "rows", None),
            P(None, "rows"),
        ),
        out_specs=P("tm", "rows", None, None),
        check_vma=False,
    )
```

```python
import jax
import jax.numpy as jnp
from jax import lax
from jax.experimental import pallas as pl
from jax.experimental.pallas import tpu as pltpu
from jax.sharding import PartitionSpec as P

MESH = pl.DeviceIdType.MESH
BF16 = jnp.bfloat16
F32 = jnp.float32
HIGH = lax.Precision.HIGHEST

CH = 768
OWN = 48
FRAMES = 3
PLANE = 256
TAPS = 9 * OWN
COUNT = 48 * 16 * 16 * 24
NT = (((1,), (1,)), ((), ()))


def iota(shape, axis):
    return lax.broadcasted_iota(jnp.int32, shape, axis)


def loop(count, body):
    def step(i, carry):
        body(i)
        return carry

    lax.fori_loop(0, count, step, 0)


def push(src, dst, send_sem, recv_sem, device):
    pltpu.make_async_remote_copy(
        src_ref=src,
        dst_ref=dst,
        send_sem=send_sem,
        recv_sem=recv_sem,
        device_id=device,
        device_id_type=MESH,
    ).start()


def await_recv(ref, sem):
    pltpu.make_async_copy(ref, ref, sem).wait()


def combine(taps):
    lane = iota((OWN, PLANE), 1)
    column = lane & 15
    total = None
    for tap_row in range(3):
        base = tap_row * 3 * OWN
        line = taps[base + OWN : base + 2 * OWN]
        line += jnp.where(column != 0, pltpu.roll(taps[base : base + OWN], 1, 1), 0.0)
        line += jnp.where(
            column != 15, pltpu.roll(taps[base + 2 * OWN : base + 3 * OWN], PLANE - 1, 1), 0.0
        )
        if tap_row == 0:
            line = jnp.where(lane >= 16, pltpu.roll(line, 16, 1), 0.0)
        elif tap_row == 2:
            line = jnp.where(lane < PLANE - 16, pltpu.roll(line, PLANE - 16, 1), 0.0)
        total = line if total is None else total + line
    return total


def silu(value):
    return value * jax.nn.sigmoid(value)


def group_matrix(shape, group_axis):
    channel = iota(shape, 1 - group_axis)
    return ((channel * 2731) >> 16 == iota(shape, group_axis)).astype(F32)


def kernel(
    x_hbm,
    gain1_hbm,
    bias1_hbm,
    gain2_hbm,
    bias2_hbm,
    w1_hbm,
    w2_hbm,
    ek_hbm,
    out_ref,
    gain1_ref,
    bias1_ref,
    gain2_ref,
    bias2_ref,
    x_ref,
    ek_ref,
    w1,
    w2,
    xg,
    act,
    lines_one,
    hg,
    act_two,
    ekt,
    taps,
    results,
    hid,
    halo_out,
    halo_in,
    stat_rows,
    stat_tm,
    stat_two,
    norms,
    gain_columns,
    bias_columns,
    across,
    pack,
    sg,
    sem_w,
    sx_send,
    sx,
    sh_send,
    sh,
    se_send,
    se,
    sstat_send,
    sstat,
    shalo_send,
    shalo,
    sg_send,
    sg_recv,
    so_send,
    so_recv,
):
    t = lax.axis_index("tm")
    r = lax.axis_index("rows")
    xh = r // 8
    z = lax.rem(r, 8)
    half = lax.rem(t, 2)

    def slot(other, distance):
        line = 1 - xh if other else xh
        return line * 8 + lax.rem(z + distance + 8, 8)


    partner = (t, slot(True, 0))
    sibling = (t + 1 - 2 * half, r)

    lines = ((True, 4), (True, 3), (True, -3), (False, 4), (True, 2), (True, -2), (False, 3), (False, -3))
    lines += ((True, 1), (True, -1), (True, 0), (False, 2), (False, -2), (False, 1), (False, -1))
    row_peers = [slot(other, distance) for other, distance in lines]
    block, plane = t // 8, lax.rem(t, 8) // 2
    steps = ((1, 2), (0, 2), (1, 1), (1, 3), (0, 1), (0, 3), (1, 0))
    tm_peers = [
        lax.rem(block + across_x, 2) * 8 + lax.rem(plane + up_y, 4) * 2 + core
        for across_x, up_y in steps
        for core in range(2)
    ] + [t + 1 - 2 * half]

    load_x = pltpu.make_async_copy(x_hbm, x_ref, sem_w.at[0])
    load_e = pltpu.make_async_copy(ek_hbm, ek_ref, sem_w.at[1])
    load1 = pltpu.make_async_copy(w1_hbm, w1, sem_w.at[2])
    load2 = pltpu.make_async_copy(w2_hbm, w2, sem_w.at[3])
    load_small = [
        pltpu.make_async_copy(src, dst, sem_w.at[4 + i])
        for i, (src, dst) in enumerate(
            (
                (gain1_hbm, gain1_ref),
                (bias1_hbm, bias1_ref),
                (gain2_hbm, gain2_ref),
                (bias2_hbm, bias2_ref),
            )
        )
    ]
    for load in [load_x, load_e, load1, load2] + load_small:
        load.start()

    barrier = pltpu.get_barrier_semaphore()

    for peer in row_peers:
        pl.semaphore_signal(barrier, inc=1, device_id=(t, peer), device_id_type=MESH)
    for peer in tm_peers:
        pl.semaphore_signal(barrier, inc=1, device_id=(peer, r), device_id_type=MESH)

    load_x.wait()
    for load in load_small:
        load.wait()
    for frame in range(FRAMES):
        xg[frame, pl.ds(pl.multiple_of(r * 16, 16), 16)] = x_ref[
            frame * 16 : frame * 16 + 16
        ]
    own = x_ref[...].astype(F32)
    row8 = iota((8, CH), 0)
    sums = jnp.where(
        row8 == 0,
        jnp.sum(own, axis=0, keepdims=True),
        jnp.where(row8 == 1, jnp.sum(own * own, axis=0, keepdims=True), 0.0),
    )
    stat_rows[r] = jnp.dot(
        sums, group_matrix((CH, 128), 1), precision=HIGH, preferred_element_type=F32
    )

    @pl.when(t == 0)
    def _():
        halo_in[...] = jnp.zeros_like(halo_in)

    pl.semaphore_wait(barrier, 30)

    def tell_rows(ref, place):
        for peer in row_peers:
            push(ref, ref, sstat_send.at[place], sstat.at[place], (t, peer))

    def tell_tm(ref, place):
        for peer in tm_peers:
            push(ref, ref, sstat_send.at[place], sstat.at[place], (peer, r))

    tell_rows(stat_rows.at[r], 0)

    plan = [
        (False, 0, ("x", 2, -2, 1, -1)),
        (False, -2, (2, 1, "x")),
        (False, 2, (-1, "x")),
        (False, -1, ("x",)),
        (False, 1, ("x",)),
        (False, -3, ("x",)),
        (False, 3, ("x",)),
        (False, -4, ("x",)),
    ] + [(True, distance, ()) for distance in (0, -2, 2, -1, 1, -3, 3, -4)]

    def ring(view, send_sem, sems, hooks, ready, arrived):
        for place, (other, distance, targets) in enumerate(plan):
            which = slot(other, distance)
            devices = [partner if to == "x" else (t, slot(False, to)) for to in targets]

            def piece(i, which=which, devices=devices, place=place):
                frame = FRAMES - 1 - i
                ref = view(which, pl.ds(frame, 1))
                if place:
                    await_recv(ref, sems.at[which, frame])
                for device in devices:
                    push(ref, ref, send_sem, sems.at[which, frame], device)

            loop(FRAMES, piece)
            if place in hooks:
                hooks[place]()
            if place == 7:
                ready()
                loop(8, lambda i: arrived(xh * 8 + i))
            elif place > 7:
                arrived(which)

    def view_x(which, frames):
        return xg.at[frames, pl.ds(pl.multiple_of(which * 16, 16), 16)]

    def view_h(which, frames):
        return hg.at[frames, pl.ds(pl.multiple_of(which * OWN, 16), OWN)]

    def exchange_tm():
        await_recv(stat_rows.at[pl.ds(0, 15)], sstat.at[0])
        stat_tm[t] = jnp.sum(stat_rows[...], axis=0)

        tell_tm(stat_tm.at[t], 1)

    def expand_prepare():
        load_e.wait()
        row = iota((384, 384), 0)
        place = (iota((384, 384), 1) == 12 * (row & 31) + (row >> 5)).astype(BF16)
        turned = lax.dot_general(place, ek_ref[...], NT, preferred_element_type=F32).astype(BF16)
        for sub in range(12):
            ekt[sub, pl.ds(pl.multiple_of(z * 32, 32), 32)] = turned[sub * 32 : sub * 32 + 32]

    def view_e(part, which):
        return ekt.at[pl.ds(part * 6, 6), pl.ds(pl.multiple_of(which * 32, 32), 32)]

    def send_e(which, device):
        ref = view_e(half, which)
        push(ref, ref, se_send, se.at[half, which], device)

    up = (t, slot(False, 1))
    down = (t, slot(False, -1))
    def expand_start():
        send_e(z, up)
        send_e(z, down)

    def expand_step(step):
        for sign, last in ((-1, 4), (1, 3)):
            if step > last:
                continue
            which = lax.rem(z + sign * step + 8, 8)
            await_recv(view_e(half, which), se.at[half, which])
            if step < last:
                send_e(which, up if sign == -1 else down)
            send_e(which, sibling)

    def expand_last(i):
        which = lax.rem(z + 1 + i, 8)
        await_recv(view_e(1 - half, which), se.at[1 - half, which])

    row8 = iota((8, 128), 0)

    def ready_one():
        await_recv(stat_tm.at[pl.ds(0, 15)], sstat.at[1])
        averages = jnp.sum(stat_tm[...], axis=0) * (1.0 / COUNT)
        mean, square = averages[0:1], averages[1:2]
        inverse = lax.rsqrt(square - mean * mean + 1e-06)
        spreads = jnp.where(row8 == 0, mean, jnp.where(row8 == 1, inverse, 0.0))
        per_channel = jnp.dot(
            spreads, group_matrix((128, CH), 0), precision=HIGH, preferred_element_type=F32
        )
        lines_one[0] = jnp.broadcast_to(per_channel[0:1], (8, CH))
        lines_one[1] = jnp.broadcast_to(per_channel[1:2] * gain1_ref[...].reshape(1, CH), (8, CH))
        lines_one[2] = jnp.broadcast_to(bias1_ref[...].reshape(1, CH), (8, CH))

    def arrived_one(which):
        part = pl.ds(pl.multiple_of(which * 16, 16), 16)
        mean, scale, bias = (lines_one[i, 0:1] for i in range(3))

        def activate(frame):
            act[frame, part] = silu((xg[frame, part].astype(F32) - mean) * scale + bias).astype(BF16)

        loop(FRAMES, activate)

    ring(
        view_x,
        sx_send,
        sx,
        {0: expand_prepare, 3: exchange_tm, 7: expand_start},
        ready_one,
        arrived_one,
    )
    expand_step(1)

    to_next = (lax.rem(t + 1, 16), r)

    def convolve(weights, product, which, between):
        def result(i):
            out_frame = 4 - i
            first = jnp.maximum(out_frame - 2, 0)
            taps[...] = jnp.zeros_like(taps)

            def step(frame, carry):
                tap_time = frame + 2 - out_frame
                rows = weights[pl.ds(pl.multiple_of(tap_time * TAPS, 16), TAPS)]
                taps[...] += product(rows, frame)
                return carry

            lax.fori_loop(first, jnp.minimum(out_frame, 2) + 1, step, 0)
            return combine(taps)

        def ahead(i):
            place = 1 - i
            halo_out[which, place] = result(i)

            @pl.when(t < 15)
            def _():
                push(
                    halo_out.at[which, place],
                    halo_in.at[which, place],
                    shalo_send.at[which],
                    shalo.at[which],
                    to_next,
                )

        def own(i):
            results[2 - i] = result(i + 2)

        loop(2, ahead)
        between()
        loop(3, own)

        @pl.when(t > 0)
        def _():
            await_recv(halo_in.at[which], shalo.at[which])

        return [
            results[0] + halo_in[which, 0],
            results[1] + halo_in[which, 1],
            results[2],
        ]

    def product_one(rows, frame):
        return lax.dot_general(rows, act[frame], NT, preferred_element_type=F32)

    def product_two(rows, frame):
        return jnp.dot(rows, act_two[frame], preferred_element_type=F32)

    load1.wait()
    hidden = [
        value.astype(BF16) for value in convolve(w1, product_one, 0, lambda: None)
    ]
    for frame in range(FRAMES):
        hg[frame, pl.ds(pl.multiple_of(r * OWN, 16), OWN)] = hidden[frame]
    hidden = [value.astype(F32) for value in hidden]

    added = hidden[0] + hidden[1] + hidden[2]
    squared = hidden[0] * hidden[0] + hidden[1] * hidden[1] + hidden[2] * hidden[2]
    lines = []
    for field in (added, squared):
        field = field[:, :128] + field[:, 128:]
        for group in range(2):
            lines.append(jnp.sum(field[group * 24 : group * 24 + 24], axis=0, keepdims=True))
    message = jnp.zeros((8, 128), F32)
    for i, line in enumerate(lines):
        message = jnp.where(row8 == i, line, message)
    stat_two[t] = message

    def residuals():
        tell_tm(stat_two.at[t], 2)
        pick = (iota((OWN, CH), 1) == r * OWN + iota((OWN, CH), 0)).astype(BF16)
        for frame in range(FRAMES):
            hid[frame] = lax.dot_general(
                pick, xg[frame], NT, preferred_element_type=F32
            )
        gain_columns[...] = jnp.broadcast_to(gain2_ref[...].reshape(1, CH), (128, CH)).T
        bias_columns[...] = jnp.broadcast_to(bias2_ref[...].reshape(1, CH), (128, CH)).T

    def spread_two():
        await_recv(stat_two.at[pl.ds(0, 15)], sstat.at[2])
        averages = jnp.sum(jnp.sum(stat_two[...], axis=0), axis=1, keepdims=True) * (1.0 / COUNT)
        averages = jnp.broadcast_to(averages, (8, 128))
        mean = averages[0:2]
        inverse = lax.rsqrt(averages[2:4] - mean * mean + 1e-06)
        norms[r] = jnp.where(
            row8 == 0,
            mean[0:1],
            jnp.where(row8 == 1, mean[1:2], jnp.where(row8 == 2, inverse[0:1], inverse[1:2])),
        )

        tell_rows(norms.at[r], 3)

    lower = iota((OWN, 128), 0) < 24

    def ready_two():
        await_recv(norms.at[pl.ds(0, 15)], sstat.at[3])

    def arrived_two(which):
        channels = pl.ds(pl.multiple_of(which * OWN, 16), OWN)
        norm = norms[which]
        mean = jnp.where(lower, norm[0:1], norm[1:2])
        scale = jnp.where(lower, norm[2:3], norm[3:4]) * gain_columns[channels]
        bias = bias_columns[channels]

        def activate(frame):
            value = hg[frame, channels].astype(F32)
            act_two[frame, channels] = jnp.concatenate(
                [
                    silu((value[:, part * 128 : part * 128 + 128] - mean) * scale + bias)
                    for part in range(2)
                ],
                axis=1,
            ).astype(BF16)

        loop(FRAMES, activate)

    ring(
        view_h,
        sh_send,
        sh,
        {0: residuals, 3: spread_two, 7: lambda: expand_step(2)},
        ready_two,
        arrived_two,
    )

    load2.wait()
    sums = convolve(w2, product_two, 1, lambda: expand_step(3))
    for frame in range(FRAMES):
        hid[frame] = (sums[frame] + hid[frame]).astype(BF16).astype(F32)

    lane = iota((OWN, 128), 1)
    for line in range(8):
        total = jnp.zeros((OWN, 128), F32)
        for part in range(2):
            for frame in range(FRAMES):
                place = 3 * part + frame
                moved = pltpu.roll(
                    hid[frame, :, part * 128 : part * 128 + 128], (16 * (place - line)) % 128, 1
                )
                total = jnp.where(lane >> 4 == place, moved, total)
        pack[line] = total.astype(BF16)
    mine = pl.ds(pl.multiple_of(r * OWN, 16), OWN)
    sg[mine] = pack[z]

    for peer in row_peers:
        push(pack.at[lax.rem(peer, 8)], sg.at[mine], sg_send, sg_recv, (t, peer))
    expand_step(4)
    loop(7, expand_last)
    column = iota((128, 128), 1)
    inside = ((column >> 5) << 4) + ((column & 31) >> 1)

    def double(line):
        return ((iota((128, 128), 0) == 48 * line + inside) & (column < 96)).astype(BF16)

    doubles = [double(1 - xh), double(xh)]
    even = (iota((256, 128), 1) & 1) == 0
    own_half = pl.ds(pl.multiple_of(xh * 256, 256), 256)
    other_half = pl.ds(pl.multiple_of(256 - xh * 256, 256), 256)
    await_recv(sg.at[pl.ds(0, 15 * OWN)], sg_recv)

    spread = [
        jnp.dot(sg[...], matrix, preferred_element_type=F32).astype(BF16) for matrix in doubles
    ]

    def rows_of(i, positions):
        both = jnp.dot(
            ekt[pl.ds(2 * i, 2)].reshape(512, CH), positions, preferred_element_type=F32
        )
        return jnp.where(even, both[:256], both[256:]).T.astype(BF16)

    def expand_other(i):
        turned = rows_of(i, spread[0])
        for frame in range(FRAMES):
            across[i, frame] = turned[frame * 32 : frame * 32 + 32]
        push(
            across.at[i],
            out_ref.at[:, i // 2, lax.rem(i, 2), :, own_half],
            so_send,
            so_recv,
            partner,
        )

    def expand_own(i):
        turned = rows_of(i, spread[1])
        for frame in range(FRAMES):
            out_ref[frame, i // 2, lax.rem(i, 2), :, own_half] = turned[
                frame * 32 : frame * 32 + 32
            ]

    loop(6, expand_other)
    loop(6, expand_own)
    await_recv(out_ref.at[:, :, :, :, other_half], so_recv)

    await_recv(xg.at[:, pl.ds(0, 15 * 16)], sx_send)
    await_recv(hg.at[:, pl.ds(0, 15 * OWN)], sh_send)
    for _ in range(2):
        await_recv(ekt.at[pl.ds(0, 6), pl.ds(0, 224)], se_send)
    await_recv(norms.at[pl.ds(0, 15)], sstat_send.at[3])
    await_recv(across, so_send)
    await_recv(stat_rows.at[pl.ds(0, 15)], sstat_send.at[0])
    await_recv(stat_tm.at[pl.ds(0, 15)], sstat_send.at[1])
    await_recv(stat_two.at[pl.ds(0, 15)], sstat_send.at[2])
    await_recv(sg.at[pl.ds(0, 15 * OWN)], sg_send)

    @pl.when(t < 15)
    def _():
        await_recv(halo_out.at[0], shalo_send.at[0])
        await_recv(halo_out.at[1], shalo_send.at[1])


def shards(
    latents,
    first_gain,
    first_bias,
    second_gain,
    second_bias,
    first_kernel,
    second_kernel,
    expand_kernel,
):
    vmem = pl.BlockSpec(memory_space=pltpu.VMEM)
    anywhere = pl.BlockSpec(memory_space=pl.ANY)
    dma = pltpu.SemaphoreType.DMA
    return pl.pallas_call(
        kernel,
        out_shape=jax.ShapeDtypeStruct((FRAMES, 3, 2, 32, 512), BF16),
        in_specs=[anywhere] * 8,
        out_specs=vmem,
        scratch_shapes=[pltpu.VMEM((CH,), F32)] * 4
        + [
            pltpu.VMEM((48, CH), BF16),
            pltpu.VMEM((CH, 384), BF16),
            pltpu.VMEM((27 * OWN, CH), BF16),
            pltpu.VMEM((27 * OWN, CH), BF16),
            pltpu.VMEM((FRAMES, PLANE, CH), BF16),
            pltpu.VMEM((FRAMES, PLANE, CH), BF16),
            pltpu.VMEM((3, 8, CH), F32),
            pltpu.VMEM((FRAMES, CH, PLANE), BF16),
            pltpu.VMEM((FRAMES, CH, PLANE), BF16),
            pltpu.VMEM((12, 256, CH), BF16),
            pltpu.VMEM((TAPS, PLANE), F32),
            pltpu.VMEM((FRAMES, OWN, PLANE), F32),
            pltpu.VMEM((FRAMES, OWN, PLANE), F32),
            pltpu.VMEM((2, 2, OWN, PLANE), F32),
            pltpu.VMEM((2, 2, OWN, PLANE), F32),
            pltpu.VMEM((16, 8, 128), F32),
            pltpu.VMEM((16, 8, 128), F32),
            pltpu.VMEM((16, 8, 128), F32),
            pltpu.VMEM((16, 8, 128), F32),
            pltpu.VMEM((CH, 128), F32),
            pltpu.VMEM((CH, 128), F32),
            pltpu.VMEM((6, FRAMES, 32, 256), BF16),
            pltpu.VMEM((8, OWN, 128), BF16),
            pltpu.VMEM((CH, 128), BF16),
            dma((8,)),
            dma,
            dma((16, FRAMES)),
            dma,
            dma((16, FRAMES)),
            dma,
            dma((2, 8)),
            dma((4,)),
            dma((4,)),
            dma((2,)),
            dma((2,)),
            dma,
            dma,
            dma,
            dma,
        ],
        compiler_params=pltpu.CompilerParams(
            collective_id=0, has_side_effects=True, vmem_limit_bytes=60 << 20
        ),
        name="block",
    )(
        latents.reshape(48, CH),
        first_gain,
        first_bias,
        second_gain,
        second_bias,
        first_kernel.reshape(27 * OWN, CH),
        second_kernel.reshape(27 * OWN, CH),
        expand_kernel,
    ).reshape(3 * FRAMES, 2, 32, 512)


def solution(mesh):
    return jax.shard_map(
        shards,
        mesh=mesh,
        in_specs=(
            P("tm", "rows", None, None),
            P(),
            P(),
            P(),
            P(),
            P(None, None, None, "rows", None),
            P(None, None, None, "rows", None),
            P(None, "rows"),
        ),
        out_specs=P("tm", "rows", None, None),
        check_vma=False,
    )
```

```python
import jax
import jax.numpy as jnp
from jax import lax
from jax.experimental import pallas as pl
from jax.experimental.pallas import tpu as pltpu
from jax.sharding import PartitionSpec as P

MESH = pl.DeviceIdType.MESH
BF16 = jnp.bfloat16
F32 = jnp.float32
HIGH = lax.Precision.HIGHEST

CH = 768
OWN = 48
FRAMES = 3
PLANE = 256
TAPS = 9 * OWN
COUNT = 48 * 16 * 16 * 24
NT = (((1,), (1,)), ((), ()))


def iota(shape, axis):
    return lax.broadcasted_iota(jnp.int32, shape, axis)


def loop(count, body):
    def step(i, carry):
        body(i)
        return carry

    lax.fori_loop(0, count, step, 0)


def push(src, dst, send_sem, recv_sem, device):
    pltpu.make_async_remote_copy(
        src_ref=src,
        dst_ref=dst,
        send_sem=send_sem,
        recv_sem=recv_sem,
        device_id=device,
        device_id_type=MESH,
    ).start()


def await_recv(ref, sem):
    pltpu.make_async_copy(ref, ref, sem).wait()


def combine(taps):
    lane = iota((OWN, PLANE), 1)
    column = lane & 15
    total = None
    for tap_row in range(3):
        base = tap_row * 3 * OWN
        line = taps[base + OWN : base + 2 * OWN]
        line += jnp.where(column != 0, pltpu.roll(taps[base : base + OWN], 1, 1), 0.0)
        line += jnp.where(
            column != 15, pltpu.roll(taps[base + 2 * OWN : base + 3 * OWN], PLANE - 1, 1), 0.0
        )
        if tap_row == 0:
            line = jnp.where(lane >= 16, pltpu.roll(line, 16, 1), 0.0)
        elif tap_row == 2:
            line = jnp.where(lane < PLANE - 16, pltpu.roll(line, PLANE - 16, 1), 0.0)
        total = line if total is None else total + line
    return total


def silu(value):
    return value * jax.nn.sigmoid(value)


def group_matrix(shape, group_axis):
    channel = iota(shape, 1 - group_axis)
    return ((channel * 2731) >> 16 == iota(shape, group_axis)).astype(F32)


def kernel(
    x_hbm,
    gain1_hbm,
    bias1_hbm,
    gain2_hbm,
    bias2_hbm,
    w1_hbm,
    w2_hbm,
    ek_hbm,
    out_ref,
    gain1_ref,
    bias1_ref,
    gain2_ref,
    bias2_ref,
    x_ref,
    ek_ref,
    w1,
    w2,
    xg,
    act,
    lines_one,
    hg,
    act_two,
    ekt,
    taps,
    results,
    hid,
    halo_out,
    halo_in,
    stat_rows,
    stat_tm,
    stat_two,
    norms,
    gain_columns,
    bias_columns,
    across,
    pack,
    sg,
    sem_w,
    sx_send,
    sx,
    sh_send,
    sh,
    se_send,
    se,
    sstat_send,
    sstat,
    shalo_send,
    shalo,
    sg_send,
    sg_recv,
    so_send,
    so_recv,
):
    t = lax.axis_index("tm")
    r = lax.axis_index("rows")
    xh = r // 8
    z = lax.rem(r, 8)
    half = lax.rem(t, 2)

    def slot(other, distance):
        line = 1 - xh if other else xh
        return line * 8 + lax.rem(z + distance + 8, 8)


    partner = (t, slot(True, 0))
    sibling = (t + 1 - 2 * half, r)

    lines = ((True, 4), (True, 3), (True, -3), (False, 4), (True, 2), (True, -2), (False, 3), (False, -3))
    lines += ((True, 1), (True, -1), (True, 0), (False, 2), (False, -2), (False, 1), (False, -1))
    row_peers = [slot(other, distance) for other, distance in lines]
    block, plane = t // 8, lax.rem(t, 8) // 2
    steps = ((1, 2), (0, 2), (1, 1), (1, 3), (0, 1), (0, 3), (1, 0))
    tm_peers = [
        lax.rem(block + across_x, 2) * 8 + lax.rem(plane + up_y, 4) * 2 + core
        for across_x, up_y in steps
        for core in range(2)
    ] + [t + 1 - 2 * half]

    load_x = pltpu.make_async_copy(x_hbm, x_ref, sem_w.at[0])
    load_e = pltpu.make_async_copy(ek_hbm, ek_ref, sem_w.at[1])
    load1 = pltpu.make_async_copy(w1_hbm, w1, sem_w.at[2])
    load2 = pltpu.make_async_copy(w2_hbm, w2, sem_w.at[3])
    load_small = [
        pltpu.make_async_copy(src, dst, sem_w.at[4 + i])
        for i, (src, dst) in enumerate(
            (
                (gain1_hbm, gain1_ref),
                (bias1_hbm, bias1_ref),
                (gain2_hbm, gain2_ref),
                (bias2_hbm, bias2_ref),
            )
        )
    ]
    for load in [load_x, load_e, load1, load2] + load_small:
        load.start()

    barrier = pltpu.get_barrier_semaphore()

    for peer in row_peers:
        pl.semaphore_signal(barrier, inc=1, device_id=(t, peer), device_id_type=MESH)
    for peer in tm_peers:
        pl.semaphore_signal(barrier, inc=1, device_id=(peer, r), device_id_type=MESH)

    load_x.wait()
    for load in load_small:
        load.wait()
    for frame in range(FRAMES):
        xg[frame, pl.ds(pl.multiple_of(r * 16, 16), 16)] = x_ref[
            frame * 16 : frame * 16 + 16
        ]
    own = x_ref[...].astype(F32)
    row8 = iota((8, CH), 0)
    sums = jnp.where(
        row8 == 0,
        jnp.sum(own, axis=0, keepdims=True),
        jnp.where(row8 == 1, jnp.sum(own * own, axis=0, keepdims=True), 0.0),
    )
    stat_rows[r] = jnp.dot(
        sums, group_matrix((CH, 128), 1), precision=HIGH, preferred_element_type=F32
    )

    @pl.when(t == 0)
    def _():
        halo_in[...] = jnp.zeros_like(halo_in)

    pl.semaphore_wait(barrier, 30)

    def tell_rows(ref, place):
        for peer in row_peers:
            push(ref, ref, sstat_send.at[place], sstat.at[place], (t, peer))

    def tell_tm(ref, place):
        for peer in tm_peers:
            push(ref, ref, sstat_send.at[place], sstat.at[place], (peer, r))

    tell_rows(stat_rows.at[r], 0)

    plan = [
        (False, 0, ("x", 2, -2, 1, -1)),
        (False, -2, (2, 1, "x")),
        (False, 2, (-1, "x")),
        (False, -1, ("x",)),
        (False, 1, ("x",)),
        (False, -3, ("x",)),
        (False, 3, ("x",)),
        (False, -4, ("x",)),
    ] + [(True, distance, ()) for distance in (0, -2, 2, -1, 1, -3, 3, -4)]

    def start_frame(view, send_sem, sems, frame):
        ref = view(r, pl.ds(frame, 1))
        for to in plan[0][2]:
            device = partner if to == "x" else (t, slot(False, to))
            push(ref, ref, send_sem, sems.at[r, frame], device)

    def ring(view, send_sem, sems, hooks, ready, arrived, begun=0):
        for place, (other, distance, targets) in enumerate(plan):
            which = slot(other, distance)
            devices = [partner if to == "x" else (t, slot(False, to)) for to in targets]

            def piece(i, which=which, devices=devices, place=place):
                frame = FRAMES - 1 - i
                ref = view(which, pl.ds(frame, 1))
                if place:
                    await_recv(ref, sems.at[which, frame])
                for device in devices:
                    push(ref, ref, send_sem, sems.at[which, frame], device)

            if place == 0 and begun:
                loop(FRAMES - begun, lambda i, piece=piece: piece(i + begun))
            else:
                loop(FRAMES, piece)
            if place in hooks:
                hooks[place]()
            if place == 7:
                ready()
                loop(8, lambda i: arrived(xh * 8 + i))
            elif place > 7:
                arrived(which)

    def view_x(which, frames):
        return xg.at[frames, pl.ds(pl.multiple_of(which * 16, 16), 16)]

    def view_h(which, frames):
        return hg.at[frames, pl.ds(pl.multiple_of(which * OWN, 16), OWN)]

    def exchange_tm():
        await_recv(stat_rows.at[pl.ds(0, 15)], sstat.at[0])
        stat_tm[t] = jnp.sum(stat_rows[...], axis=0)

        tell_tm(stat_tm.at[t], 1)

    def expand_prepare():
        load_e.wait()
        row = iota((384, 384), 0)
        place = (iota((384, 384), 1) == 12 * (row & 31) + (row >> 5)).astype(BF16)
        turned = lax.dot_general(place, ek_ref[...], NT, preferred_element_type=F32).astype(BF16)
        for sub in range(12):
            ekt[sub, pl.ds(pl.multiple_of(z * 32, 32), 32)] = turned[sub * 32 : sub * 32 + 32]

    def view_e(part, which):
        return ekt.at[pl.ds(part * 6, 6), pl.ds(pl.multiple_of(which * 32, 32), 32)]

    def send_e(which, device):
        ref = view_e(half, which)
        push(ref, ref, se_send, se.at[half, which], device)

    up = (t, slot(False, 1))
    down = (t, slot(False, -1))
    def expand_start():
        send_e(z, up)
        send_e(z, down)

    def expand_step(step):
        for sign, last in ((-1, 4), (1, 3)):
            if step > last:
                continue
            which = lax.rem(z + sign * step + 8, 8)
            await_recv(view_e(half, which), se.at[half, which])
            if step < last:
                send_e(which, up if sign == -1 else down)
            send_e(which, sibling)

    def expand_last(i):
        which = lax.rem(z + 1 + i, 8)
        await_recv(view_e(1 - half, which), se.at[1 - half, which])

    row8 = iota((8, 128), 0)

    def ready_one():
        await_recv(stat_tm.at[pl.ds(0, 15)], sstat.at[1])
        averages = jnp.sum(stat_tm[...], axis=0) * (1.0 / COUNT)
        mean, square = averages[0:1], averages[1:2]
        inverse = lax.rsqrt(square - mean * mean + 1e-06)
        spreads = jnp.where(row8 == 0, mean, jnp.where(row8 == 1, inverse, 0.0))
        per_channel = jnp.dot(
            spreads, group_matrix((128, CH), 0), precision=HIGH, preferred_element_type=F32
        )
        lines_one[0] = jnp.broadcast_to(per_channel[0:1], (8, CH))
        lines_one[1] = jnp.broadcast_to(per_channel[1:2] * gain1_ref[...].reshape(1, CH), (8, CH))
        lines_one[2] = jnp.broadcast_to(bias1_ref[...].reshape(1, CH), (8, CH))

    def arrived_one(which):
        part = pl.ds(pl.multiple_of(which * 16, 16), 16)
        mean, scale, bias = (lines_one[i, 0:1] for i in range(3))

        def activate(frame):
            act[frame, part] = silu((xg[frame, part].astype(F32) - mean) * scale + bias).astype(BF16)

        loop(FRAMES, activate)

    ring(
        view_x,
        sx_send,
        sx,
        {0: expand_prepare, 3: exchange_tm, 7: expand_start},
        ready_one,
        arrived_one,
    )
    expand_step(1)

    to_next = (lax.rem(t + 1, 16), r)

    def convolve(weights, product, which, between, early):
        def result(i):
            out_frame = 4 - i
            first = jnp.maximum(out_frame - 2, 0)
            taps[...] = jnp.zeros_like(taps)

            def step(frame, carry):
                tap_time = frame + 2 - out_frame
                rows = weights[pl.ds(pl.multiple_of(tap_time * TAPS, 16), TAPS)]
                taps[...] += product(rows, frame)
                return carry

            lax.fori_loop(first, jnp.minimum(out_frame, 2) + 1, step, 0)
            return combine(taps)

        def ahead(i):
            place = 1 - i
            halo_out[which, place] = result(i)

            @pl.when(t < 15)
            def _():
                push(
                    halo_out.at[which, place],
                    halo_in.at[which, place],
                    shalo_send.at[which],
                    shalo.at[which],
                    to_next,
                )

        def own(i):
            results[2 - i] = result(i + 2)

        loop(2, ahead)
        between()
        loop(3, own)
        early()

        @pl.when(t > 0)
        def _():
            await_recv(halo_in.at[which], shalo.at[which])

        return [
            results[0] + halo_in[which, 0],
            results[1] + halo_in[which, 1],
            results[2],
        ]

    def product_one(rows, frame):
        return lax.dot_general(rows, act[frame], NT, preferred_element_type=F32)

    def product_two(rows, frame):
        return jnp.dot(rows, act_two[frame], preferred_element_type=F32)

    def first_frame():
        hg[2, pl.ds(pl.multiple_of(r * OWN, 16), OWN)] = results[2].astype(BF16)
        start_frame(view_h, sh_send, sh, 2)

    load1.wait()
    hidden = [
        value.astype(BF16) for value in convolve(w1, product_one, 0, lambda: None, first_frame)
    ]
    for frame in range(FRAMES - 1):
        hg[frame, pl.ds(pl.multiple_of(r * OWN, 16), OWN)] = hidden[frame]
    hidden = [value.astype(F32) for value in hidden]

    added = hidden[0] + hidden[1] + hidden[2]
    squared = hidden[0] * hidden[0] + hidden[1] * hidden[1] + hidden[2] * hidden[2]
    lines = []
    for field in (added, squared):
        field = field[:, :128] + field[:, 128:]
        for group in range(2):
            lines.append(jnp.sum(field[group * 24 : group * 24 + 24], axis=0, keepdims=True))
    message = jnp.zeros((8, 128), F32)
    for i, line in enumerate(lines):
        message = jnp.where(row8 == i, line, message)
    stat_two[t] = message

    def residuals():
        tell_tm(stat_two.at[t], 2)
        pick = (iota((OWN, CH), 1) == r * OWN + iota((OWN, CH), 0)).astype(BF16)
        for frame in range(FRAMES):
            hid[frame] = lax.dot_general(
                pick, xg[frame], NT, preferred_element_type=F32
            )
        gain_columns[...] = jnp.broadcast_to(gain2_ref[...].reshape(1, CH), (128, CH)).T
        bias_columns[...] = jnp.broadcast_to(bias2_ref[...].reshape(1, CH), (128, CH)).T

    def spread_two():
        await_recv(stat_two.at[pl.ds(0, 15)], sstat.at[2])
        averages = jnp.sum(jnp.sum(stat_two[...], axis=0), axis=1, keepdims=True) * (1.0 / COUNT)
        averages = jnp.broadcast_to(averages, (8, 128))
        mean = averages[0:2]
        inverse = lax.rsqrt(averages[2:4] - mean * mean + 1e-06)
        norms[r] = jnp.where(
            row8 == 0,
            mean[0:1],
            jnp.where(row8 == 1, mean[1:2], jnp.where(row8 == 2, inverse[0:1], inverse[1:2])),
        )

        tell_rows(norms.at[r], 3)

    lower = iota((OWN, 128), 0) < 24

    def ready_two():
        await_recv(norms.at[pl.ds(0, 15)], sstat.at[3])

    def arrived_two(which):
        channels = pl.ds(pl.multiple_of(which * OWN, 16), OWN)
        norm = norms[which]
        mean = jnp.where(lower, norm[0:1], norm[1:2])
        scale = jnp.where(lower, norm[2:3], norm[3:4]) * gain_columns[channels]
        bias = bias_columns[channels]

        def activate(frame):
            value = hg[frame, channels].astype(F32)
            act_two[frame, channels] = jnp.concatenate(
                [
                    silu((value[:, part * 128 : part * 128 + 128] - mean) * scale + bias)
                    for part in range(2)
                ],
                axis=1,
            ).astype(BF16)

        loop(FRAMES, activate)

    ring(
        view_h,
        sh_send,
        sh,
        {0: residuals, 3: spread_two, 7: lambda: expand_step(2)},
        ready_two,
        arrived_two,
        1,
    )

    load2.wait()
    sums = convolve(w2, product_two, 1, lambda: expand_step(3), lambda: None)
    for frame in range(FRAMES):
        hid[frame] = (sums[frame] + hid[frame]).astype(BF16).astype(F32)

    lane = iota((OWN, 128), 1)
    for line in range(8):
        total = jnp.zeros((OWN, 128), F32)
        for part in range(2):
            for frame in range(FRAMES):
                place = 3 * part + frame
                moved = pltpu.roll(
                    hid[frame, :, part * 128 : part * 128 + 128], (16 * (place - line)) % 128, 1
                )
                total = jnp.where(lane >> 4 == place, moved, total)
        pack[line] = total.astype(BF16)
    mine = pl.ds(pl.multiple_of(r * OWN, 16), OWN)
    sg[mine] = pack[z]

    for peer in row_peers:
        push(pack.at[lax.rem(peer, 8)], sg.at[mine], sg_send, sg_recv, (t, peer))
    expand_step(4)
    loop(7, expand_last)
    column = iota((128, 128), 1)
    inside = ((column >> 5) << 4) + ((column & 31) >> 1)

    def double(line):
        return ((iota((128, 128), 0) == 48 * line + inside) & (column < 96)).astype(BF16)

    doubles = [double(1 - xh), double(xh)]
    even = (iota((256, 128), 1) & 1) == 0
    own_half = pl.ds(pl.multiple_of(xh * 256, 256), 256)
    other_half = pl.ds(pl.multiple_of(256 - xh * 256, 256), 256)
    await_recv(sg.at[pl.ds(0, 15 * OWN)], sg_recv)

    spread = [
        jnp.dot(sg[...], matrix, preferred_element_type=F32).astype(BF16) for matrix in doubles
    ]

    def rows_of(i, positions):
        both = jnp.dot(
            ekt[pl.ds(2 * i, 2)].reshape(512, CH), positions, preferred_element_type=F32
        )
        return jnp.where(even, both[:256], both[256:]).T.astype(BF16)

    def expand_other(i):
        turned = rows_of(i, spread[0])
        for frame in range(FRAMES):
            across[i, frame] = turned[frame * 32 : frame * 32 + 32]
        push(
            across.at[i],
            out_ref.at[:, i // 2, lax.rem(i, 2), :, own_half],
            so_send,
            so_recv,
            partner,
        )

    def expand_own(i):
        turned = rows_of(i, spread[1])
        for frame in range(FRAMES):
            out_ref[frame, i // 2, lax.rem(i, 2), :, own_half] = turned[
                frame * 32 : frame * 32 + 32
            ]

    loop(6, expand_other)
    loop(6, expand_own)
    await_recv(out_ref.at[:, :, :, :, other_half], so_recv)

    await_recv(xg.at[:, pl.ds(0, 15 * 16)], sx_send)
    await_recv(hg.at[:, pl.ds(0, 15 * OWN)], sh_send)
    for _ in range(2):
        await_recv(ekt.at[pl.ds(0, 6), pl.ds(0, 224)], se_send)
    await_recv(norms.at[pl.ds(0, 15)], sstat_send.at[3])
    await_recv(across, so_send)
    await_recv(stat_rows.at[pl.ds(0, 15)], sstat_send.at[0])
    await_recv(stat_tm.at[pl.ds(0, 15)], sstat_send.at[1])
    await_recv(stat_two.at[pl.ds(0, 15)], sstat_send.at[2])
    await_recv(sg.at[pl.ds(0, 15 * OWN)], sg_send)

    @pl.when(t < 15)
    def _():
        await_recv(halo_out.at[0], shalo_send.at[0])
        await_recv(halo_out.at[1], shalo_send.at[1])


def shards(
    latents,
    first_gain,
    first_bias,
    second_gain,
    second_bias,
    first_kernel,
    second_kernel,
    expand_kernel,
):
    vmem = pl.BlockSpec(memory_space=pltpu.VMEM)
    anywhere = pl.BlockSpec(memory_space=pl.ANY)
    dma = pltpu.SemaphoreType.DMA
    return pl.pallas_call(
        kernel,
        out_shape=pltpu.VMEM((FRAMES, 3, 2, 32, 512), BF16),
        in_specs=[anywhere] * 8,
        out_specs=vmem,
        scratch_shapes=[pltpu.VMEM((CH,), F32)] * 4
        + [
            pltpu.VMEM((48, CH), BF16),
            pltpu.VMEM((CH, 384), BF16),
            pltpu.VMEM((27 * OWN, CH), BF16),
            pltpu.VMEM((27 * OWN, CH), BF16),
            pltpu.VMEM((FRAMES, PLANE, CH), BF16),
            pltpu.VMEM((FRAMES, PLANE, CH), BF16),
            pltpu.VMEM((3, 8, CH), F32),
            pltpu.VMEM((FRAMES, CH, PLANE), BF16),
            pltpu.VMEM((FRAMES, CH, PLANE), BF16),
            pltpu.VMEM((12, 256, CH), BF16),
            pltpu.VMEM((TAPS, PLANE), F32),
            pltpu.VMEM((FRAMES, OWN, PLANE), F32),
            pltpu.VMEM((FRAMES, OWN, PLANE), F32),
            pltpu.VMEM((2, 2, OWN, PLANE), F32),
            pltpu.VMEM((2, 2, OWN, PLANE), F32),
            pltpu.VMEM((16, 8, 128), F32),
            pltpu.VMEM((16, 8, 128), F32),
            pltpu.VMEM((16, 8, 128), F32),
            pltpu.VMEM((16, 8, 128), F32),
            pltpu.VMEM((CH, 128), F32),
            pltpu.VMEM((CH, 128), F32),
            pltpu.VMEM((6, FRAMES, 32, 256), BF16),
            pltpu.VMEM((8, OWN, 128), BF16),
            pltpu.VMEM((CH, 128), BF16),
            dma((8,)),
            dma,
            dma((16, FRAMES)),
            dma,
            dma((16, FRAMES)),
            dma,
            dma((2, 8)),
            dma((4,)),
            dma((4,)),
            dma((2,)),
            dma((2,)),
            dma,
            dma,
            dma,
            dma,
        ],
        compiler_params=pltpu.CompilerParams(
            collective_id=0, has_side_effects=True, vmem_limit_bytes=48 << 20
        ),
        name="block",
    )(
        *[
            pltpu.with_memory_space_constraint(array, pltpu.HBM)
            for array in (
                latents.reshape(48, CH),
                first_gain,
                first_bias,
                second_gain,
                second_bias,
                first_kernel.reshape(27 * OWN, CH),
                second_kernel.reshape(27 * OWN, CH),
                expand_kernel,
            )
        ]
    ).reshape(3 * FRAMES, 2, 32, 512)


def solution(mesh):
    return jax.shard_map(
        shards,
        mesh=mesh,
        in_specs=(
            P("tm", "rows", None, None),
            P(),
            P(),
            P(),
            P(),
            P(None, None, None, "rows", None),
            P(None, None, None, "rows", None),
            P(None, "rows"),
        ),
        out_specs=P("tm", "rows", None, None),
        check_vma=False,
    )
```

```python
import jax
import jax.numpy as jnp
from jax import lax
from jax.experimental import pallas as pl
from jax.experimental.pallas import tpu as pltpu
from jax.sharding import PartitionSpec as P

MESH = pl.DeviceIdType.MESH
BF16 = jnp.bfloat16
F32 = jnp.float32
HIGH = lax.Precision.HIGHEST

CH = 768
OWN = 48
FRAMES = 3
PLANE = 256
TAPS = 9 * OWN
COUNT = 48 * 16 * 16 * 24
NT = (((1,), (1,)), ((), ()))


def iota(shape, axis):
    return lax.broadcasted_iota(jnp.int32, shape, axis)


def loop(count, body):
    def step(i, carry):
        body(i)
        return carry

    lax.fori_loop(0, count, step, 0)


def push(src, dst, send_sem, recv_sem, device):
    pltpu.make_async_remote_copy(
        src_ref=src,
        dst_ref=dst,
        send_sem=send_sem,
        recv_sem=recv_sem,
        device_id=device,
        device_id_type=MESH,
    ).start()


def await_recv(ref, sem):
    pltpu.make_async_copy(ref, ref, sem).wait()


def combine(taps):
    lane = iota((OWN, PLANE), 1)
    column = lane & 15
    total = None
    for tap_row in range(3):
        base = tap_row * 3 * OWN
        line = taps[base + OWN : base + 2 * OWN]
        line += jnp.where(column != 0, pltpu.roll(taps[base : base + OWN], 1, 1), 0.0)
        line += jnp.where(
            column != 15, pltpu.roll(taps[base + 2 * OWN : base + 3 * OWN], PLANE - 1, 1), 0.0
        )
        if tap_row == 0:
            line = jnp.where(lane >= 16, pltpu.roll(line, 16, 1), 0.0)
        elif tap_row == 2:
            line = jnp.where(lane < PLANE - 16, pltpu.roll(line, PLANE - 16, 1), 0.0)
        total = line if total is None else total + line
    return total


def silu(value):
    return value * jax.nn.sigmoid(value)


def group_matrix(shape, group_axis):
    channel = iota(shape, 1 - group_axis)
    return ((channel * 2731) >> 16 == iota(shape, group_axis)).astype(F32)


def kernel(
    x_hbm,
    gain1_hbm,
    bias1_hbm,
    gain2_hbm,
    bias2_hbm,
    w1_hbm,
    w2_hbm,
    ek_hbm,
    out_ref,
    gain1_ref,
    bias1_ref,
    gain2_ref,
    bias2_ref,
    x_ref,
    ek_ref,
    w1,
    w2,
    xg,
    act,
    lines_one,
    hg,
    act_two,
    ekt,
    taps,
    results,
    hid,
    halo_out,
    halo_in,
    stat_rows,
    stat_tm,
    stat_two,
    norms,
    gain_columns,
    bias_columns,
    across,
    pack,
    sg,
    sem_w,
    sx_send,
    sx,
    sh_send,
    sh,
    se_send,
    se,
    sstat_send,
    sstat,
    shalo_send,
    shalo,
    sg_send,
    sg_recv,
    so_send,
    so_recv,
):
    t = lax.axis_index("tm")
    r = lax.axis_index("rows")
    xh = r // 8
    z = lax.rem(r, 8)
    half = lax.rem(t, 2)

    def slot(other, distance):
        line = 1 - xh if other else xh
        return line * 8 + lax.rem(z + distance + 8, 8)


    partner = (t, slot(True, 0))
    sibling = (t + 1 - 2 * half, r)

    lines = ((True, 4), (True, 3), (True, -3), (False, 4), (True, 2), (True, -2), (False, 3), (False, -3))
    lines += ((True, 1), (True, -1), (True, 0), (False, 2), (False, -2), (False, 1), (False, -1))
    row_peers = [slot(other, distance) for other, distance in lines]
    block, plane = t // 8, lax.rem(t, 8) // 2
    steps = ((1, 2), (0, 2), (1, 1), (1, 3), (0, 1), (0, 3), (1, 0))
    tm_peers = [
        lax.rem(block + across_x, 2) * 8 + lax.rem(plane + up_y, 4) * 2 + core
        for across_x, up_y in steps
        for core in range(2)
    ] + [t + 1 - 2 * half]

    barrier = pltpu.get_barrier_semaphore()

    for peer in row_peers:
        pl.semaphore_signal(barrier, inc=1, device_id=(t, peer), device_id_type=MESH)
    for peer in tm_peers:
        pl.semaphore_signal(barrier, inc=1, device_id=(peer, r), device_id_type=MESH)

    load_x = pltpu.make_async_copy(x_hbm, x_ref, sem_w.at[0])
    load_e = pltpu.make_async_copy(ek_hbm, ek_ref, sem_w.at[1])
    load1 = pltpu.make_async_copy(w1_hbm, w1, sem_w.at[2])
    load2 = pltpu.make_async_copy(w2_hbm, w2, sem_w.at[3])
    load_small = [
        pltpu.make_async_copy(src, dst, sem_w.at[4 + i])
        for i, (src, dst) in enumerate(
            (
                (gain1_hbm, gain1_ref),
                (bias1_hbm, bias1_ref),
                (gain2_hbm, gain2_ref),
                (bias2_hbm, bias2_ref),
            )
        )
    ]
    for load in [load_x] + load_small + [load_e, load1, load2]:
        load.start()

    load_x.wait()
    for frame in range(FRAMES):
        xg[frame, pl.ds(pl.multiple_of(r * 16, 16), 16)] = x_ref[
            frame * 16 : frame * 16 + 16
        ]
    own = x_ref[...].astype(F32)
    row8 = iota((8, CH), 0)
    sums = jnp.where(
        row8 == 0,
        jnp.sum(own, axis=0, keepdims=True),
        jnp.where(row8 == 1, jnp.sum(own * own, axis=0, keepdims=True), 0.0),
    )
    stat_rows[r] = jnp.dot(
        sums, group_matrix((CH, 128), 1), precision=HIGH, preferred_element_type=F32
    )

    @pl.when(t == 0)
    def _():
        halo_in[...] = jnp.zeros_like(halo_in)

    for load in load_small:
        load.wait()
    pl.semaphore_wait(barrier, 30)

    def tell_rows(ref, place):
        for peer in row_peers:
            push(ref, ref, sstat_send.at[place], sstat.at[place], (t, peer))

    def tell_tm(ref, place):
        for peer in tm_peers:
            push(ref, ref, sstat_send.at[place], sstat.at[place], (peer, r))

    tell_rows(stat_rows.at[r], 0)

    plan = [
        (False, 0, ("x", 2, -2, 1, -1)),
        (False, -2, (2, 1, "x")),
        (False, 2, (-1, "x")),
        (False, -1, ("x",)),
        (False, 1, ("x",)),
        (False, -3, ("x",)),
        (False, 3, ("x",)),
        (False, -4, ("x",)),
    ] + [(True, distance, ()) for distance in (0, -2, 2, -1, 1, -3, 3, -4)]

    def start_frame(view, send_sem, sems, frame):
        ref = view(r, pl.ds(frame, 1))
        for to in plan[0][2]:
            device = partner if to == "x" else (t, slot(False, to))
            push(ref, ref, send_sem, sems.at[r, frame], device)

    def ring(view, send_sem, sems, hooks, ready, arrived, begun=0):
        for place, (other, distance, targets) in enumerate(plan):
            which = slot(other, distance)
            devices = [partner if to == "x" else (t, slot(False, to)) for to in targets]

            def piece(i, which=which, devices=devices, place=place):
                frame = FRAMES - 1 - i
                ref = view(which, pl.ds(frame, 1))
                if place:
                    await_recv(ref, sems.at[which, frame])
                for device in devices:
                    push(ref, ref, send_sem, sems.at[which, frame], device)

            if place == 0 and begun:
                loop(FRAMES - begun, lambda i, piece=piece: piece(i + begun))
            else:
                loop(FRAMES, piece)
            if place in hooks:
                hooks[place]()
            if place == 7:
                ready()
                loop(8, lambda i: arrived(xh * 8 + i))
            elif place > 7:
                arrived(which)

    def view_x(which, frames):
        return xg.at[frames, pl.ds(pl.multiple_of(which * 16, 16), 16)]

    def view_h(which, frames):
        return hg.at[frames, pl.ds(pl.multiple_of(which * OWN, 16), OWN)]

    def exchange_tm():
        await_recv(stat_rows.at[pl.ds(0, 15)], sstat.at[0])
        stat_tm[t] = jnp.sum(stat_rows[...], axis=0)

        tell_tm(stat_tm.at[t], 1)

    def expand_prepare():
        load_e.wait()
        row = iota((384, 384), 0)
        place = (iota((384, 384), 1) == 12 * (row & 31) + (row >> 5)).astype(BF16)
        turned = lax.dot_general(place, ek_ref[...], NT, preferred_element_type=F32).astype(BF16)
        for sub in range(12):
            ekt[sub, pl.ds(pl.multiple_of(z * 32, 32), 32)] = turned[sub * 32 : sub * 32 + 32]

    def view_e(part, which):
        return ekt.at[pl.ds(part * 6, 6), pl.ds(pl.multiple_of(which * 32, 32), 32)]

    def send_e(which, device):
        ref = view_e(half, which)
        push(ref, ref, se_send, se.at[half, which], device)

    up = (t, slot(False, 1))
    down = (t, slot(False, -1))
    def expand_start():
        send_e(z, up)
        send_e(z, down)

    def expand_step(step):
        for sign, last in ((-1, 4), (1, 3)):
            if step > last:
                continue
            which = lax.rem(z + sign * step + 8, 8)
            await_recv(view_e(half, which), se.at[half, which])
            if step < last:
                send_e(which, up if sign == -1 else down)
            send_e(which, sibling)

    def expand_last(i):
        which = lax.rem(z + 1 + i, 8)
        await_recv(view_e(1 - half, which), se.at[1 - half, which])

    row8 = iota((8, 128), 0)

    def ready_one():
        await_recv(stat_tm.at[pl.ds(0, 15)], sstat.at[1])
        averages = jnp.sum(stat_tm[...], axis=0) * (1.0 / COUNT)
        mean, square = averages[0:1], averages[1:2]
        inverse = lax.rsqrt(square - mean * mean + 1e-06)
        spreads = jnp.where(row8 == 0, mean, jnp.where(row8 == 1, inverse, 0.0))
        per_channel = jnp.dot(
            spreads, group_matrix((128, CH), 0), precision=HIGH, preferred_element_type=F32
        )
        lines_one[0] = jnp.broadcast_to(per_channel[0:1], (8, CH))
        lines_one[1] = jnp.broadcast_to(per_channel[1:2] * gain1_ref[...].reshape(1, CH), (8, CH))
        lines_one[2] = jnp.broadcast_to(bias1_ref[...].reshape(1, CH), (8, CH))

    def arrived_one(which):
        part = pl.ds(pl.multiple_of(which * 16, 16), 16)
        mean, scale, bias = (lines_one[i, 0:1] for i in range(3))

        def activate(frame):
            act[frame, part] = silu((xg[frame, part].astype(F32) - mean) * scale + bias).astype(BF16)

        loop(FRAMES, activate)

    ring(
        view_x,
        sx_send,
        sx,
        {0: expand_prepare, 3: exchange_tm, 7: expand_start},
        ready_one,
        arrived_one,
    )
    expand_step(1)

    to_next = (lax.rem(t + 1, 16), r)

    def convolve(weights, product, which, between, early):
        def result(i):
            out_frame = 4 - i
            first = jnp.maximum(out_frame - 2, 0)
            taps[...] = jnp.zeros_like(taps)

            def step(frame, carry):
                tap_time = frame + 2 - out_frame
                rows = weights[pl.ds(pl.multiple_of(tap_time * TAPS, 16), TAPS)]
                taps[...] += product(rows, frame)
                return carry

            lax.fori_loop(first, jnp.minimum(out_frame, 2) + 1, step, 0)
            return combine(taps)

        def ahead(i):
            place = 1 - i
            halo_out[which, place] = result(i)

            @pl.when(t < 15)
            def _():
                push(
                    halo_out.at[which, place],
                    halo_in.at[which, place],
                    shalo_send.at[which],
                    shalo.at[which],
                    to_next,
                )

        def own(i):
            results[2 - i] = result(i + 2)

        loop(2, ahead)
        between()
        loop(3, own)
        early()

        @pl.when(t > 0)
        def _():
            await_recv(halo_in.at[which], shalo.at[which])

        return [
            results[0] + halo_in[which, 0],
            results[1] + halo_in[which, 1],
            results[2],
        ]

    def product_one(rows, frame):
        return lax.dot_general(rows, act[frame], NT, preferred_element_type=F32)

    def product_two(rows, frame):
        return jnp.dot(rows, act_two[frame], preferred_element_type=F32)

    def first_frame():
        hg[2, pl.ds(pl.multiple_of(r * OWN, 16), OWN)] = results[2].astype(BF16)
        start_frame(view_h, sh_send, sh, 2)

    load1.wait()
    hidden = [
        value.astype(BF16) for value in convolve(w1, product_one, 0, lambda: None, first_frame)
    ]
    for frame in range(FRAMES - 1):
        hg[frame, pl.ds(pl.multiple_of(r * OWN, 16), OWN)] = hidden[frame]
    hidden = [value.astype(F32) for value in hidden]

    added = hidden[0] + hidden[1] + hidden[2]
    squared = hidden[0] * hidden[0] + hidden[1] * hidden[1] + hidden[2] * hidden[2]
    lines = []
    for field in (added, squared):
        field = field[:, :128] + field[:, 128:]
        for group in range(2):
            lines.append(jnp.sum(field[group * 24 : group * 24 + 24], axis=0, keepdims=True))
    message = jnp.zeros((8, 128), F32)
    for i, line in enumerate(lines):
        message = jnp.where(row8 == i, line, message)
    stat_two[t] = message

    def residuals():
        tell_tm(stat_two.at[t], 2)
        pick = (iota((OWN, CH), 1) == r * OWN + iota((OWN, CH), 0)).astype(BF16)
        for frame in range(FRAMES):
            hid[frame] = lax.dot_general(
                pick, xg[frame], NT, preferred_element_type=F32
            )
        gain_columns[...] = jnp.broadcast_to(gain2_ref[...].reshape(1, CH), (128, CH)).T
        bias_columns[...] = jnp.broadcast_to(bias2_ref[...].reshape(1, CH), (128, CH)).T

    def spread_two():
        await_recv(stat_two.at[pl.ds(0, 15)], sstat.at[2])
        averages = jnp.sum(jnp.sum(stat_two[...], axis=0), axis=1, keepdims=True) * (1.0 / COUNT)
        averages = jnp.broadcast_to(averages, (8, 128))
        mean = averages[0:2]
        inverse = lax.rsqrt(averages[2:4] - mean * mean + 1e-06)
        norms[r] = jnp.where(
            row8 == 0,
            mean[0:1],
            jnp.where(row8 == 1, mean[1:2], jnp.where(row8 == 2, inverse[0:1], inverse[1:2])),
        )

        tell_rows(norms.at[r], 3)

    lower = iota((OWN, 128), 0) < 24

    def ready_two():
        await_recv(norms.at[pl.ds(0, 15)], sstat.at[3])

    def arrived_two(which):
        channels = pl.ds(pl.multiple_of(which * OWN, 16), OWN)
        norm = norms[which]
        mean = jnp.where(lower, norm[0:1], norm[1:2])
        scale = jnp.where(lower, norm[2:3], norm[3:4]) * gain_columns[channels]
        bias = bias_columns[channels]

        def activate(frame):
            value = hg[frame, channels].astype(F32)
            act_two[frame, channels] = jnp.concatenate(
                [
                    silu((value[:, part * 128 : part * 128 + 128] - mean) * scale + bias)
                    for part in range(2)
                ],
                axis=1,
            ).astype(BF16)

        loop(FRAMES, activate)

    ring(
        view_h,
        sh_send,
        sh,
        {0: residuals, 3: spread_two, 7: lambda: expand_step(2)},
        ready_two,
        arrived_two,
        1,
    )

    load2.wait()
    sums = convolve(w2, product_two, 1, lambda: expand_step(3), lambda: None)
    for frame in range(FRAMES):
        hid[frame] = (sums[frame] + hid[frame]).astype(BF16).astype(F32)

    lane = iota((OWN, 128), 1)
    for line in range(8):
        total = jnp.zeros((OWN, 128), F32)
        for part in range(2):
            for frame in range(FRAMES):
                place = 3 * part + frame
                moved = pltpu.roll(
                    hid[frame, :, part * 128 : part * 128 + 128], (16 * (place - line)) % 128, 1
                )
                total = jnp.where(lane >> 4 == place, moved, total)
        pack[line] = total.astype(BF16)
    mine = pl.ds(pl.multiple_of(r * OWN, 16), OWN)
    sg[mine] = pack[z]

    for peer in row_peers:
        push(pack.at[lax.rem(peer, 8)], sg.at[mine], sg_send, sg_recv, (t, peer))
    expand_step(4)
    loop(7, expand_last)
    column = iota((128, 128), 1)
    inside = ((column >> 5) << 4) + ((column & 31) >> 1)

    def double(line):
        return ((iota((128, 128), 0) == 48 * line + inside) & (column < 96)).astype(BF16)

    doubles = [double(1 - xh), double(xh)]
    even = (iota((256, 128), 1) & 1) == 0
    own_half = pl.ds(pl.multiple_of(xh * 256, 256), 256)
    other_half = pl.ds(pl.multiple_of(256 - xh * 256, 256), 256)
    await_recv(sg.at[pl.ds(0, 15 * OWN)], sg_recv)

    spread = [
        jnp.dot(sg[...], matrix, preferred_element_type=F32).astype(BF16) for matrix in doubles
    ]

    def rows_of(i, positions):
        both = jnp.dot(
            ekt[pl.ds(2 * i, 2)].reshape(512, CH), positions, preferred_element_type=F32
        )
        return jnp.where(even, both[:256], both[256:]).T.astype(BF16)

    def expand_other(i):
        turned = rows_of(i, spread[0])
        for frame in range(FRAMES):
            across[i, frame] = turned[frame * 32 : frame * 32 + 32]
        push(
            across.at[i],
            out_ref.at[:, i // 2, lax.rem(i, 2), :, own_half],
            so_send,
            so_recv,
            partner,
        )

    def expand_own(i):
        turned = rows_of(i, spread[1])
        for frame in range(FRAMES):
            out_ref[frame, i // 2, lax.rem(i, 2), :, own_half] = turned[
                frame * 32 : frame * 32 + 32
            ]

    loop(6, expand_other)
    loop(6, expand_own)
    await_recv(out_ref.at[:, :, :, :, other_half], so_recv)

    await_recv(xg.at[:, pl.ds(0, 15 * 16)], sx_send)
    await_recv(hg.at[:, pl.ds(0, 15 * OWN)], sh_send)
    for _ in range(2):
        await_recv(ekt.at[pl.ds(0, 6), pl.ds(0, 224)], se_send)
    await_recv(norms.at[pl.ds(0, 15)], sstat_send.at[3])
    await_recv(across, so_send)
    await_recv(stat_rows.at[pl.ds(0, 15)], sstat_send.at[0])
    await_recv(stat_tm.at[pl.ds(0, 15)], sstat_send.at[1])
    await_recv(stat_two.at[pl.ds(0, 15)], sstat_send.at[2])
    await_recv(sg.at[pl.ds(0, 15 * OWN)], sg_send)

    @pl.when(t < 15)
    def _():
        await_recv(halo_out.at[0], shalo_send.at[0])
        await_recv(halo_out.at[1], shalo_send.at[1])


def shards(
    latents,
    first_gain,
    first_bias,
    second_gain,
    second_bias,
    first_kernel,
    second_kernel,
    expand_kernel,
):
    vmem = pl.BlockSpec(memory_space=pltpu.VMEM)
    anywhere = pl.BlockSpec(memory_space=pl.ANY)
    dma = pltpu.SemaphoreType.DMA
    return pl.pallas_call(
        kernel,
        out_shape=pltpu.VMEM((FRAMES, 3, 2, 32, 512), BF16),
        in_specs=[anywhere] * 8,
        out_specs=vmem,
        scratch_shapes=[pltpu.VMEM((CH,), F32)] * 4
        + [
            pltpu.VMEM((48, CH), BF16),
            pltpu.VMEM((CH, 384), BF16),
            pltpu.VMEM((27 * OWN, CH), BF16),
            pltpu.VMEM((27 * OWN, CH), BF16),
            pltpu.VMEM((FRAMES, PLANE, CH), BF16),
            pltpu.VMEM((FRAMES, PLANE, CH), BF16),
            pltpu.VMEM((3, 8, CH), F32),
            pltpu.VMEM((FRAMES, CH, PLANE), BF16),
            pltpu.VMEM((FRAMES, CH, PLANE), BF16),
            pltpu.VMEM((12, 256, CH), BF16),
            pltpu.VMEM((TAPS, PLANE), F32),
            pltpu.VMEM((FRAMES, OWN, PLANE), F32),
            pltpu.VMEM((FRAMES, OWN, PLANE), F32),
            pltpu.VMEM((2, 2, OWN, PLANE), F32),
            pltpu.VMEM((2, 2, OWN, PLANE), F32),
            pltpu.VMEM((16, 8, 128), F32),
            pltpu.VMEM((16, 8, 128), F32),
            pltpu.VMEM((16, 8, 128), F32),
            pltpu.VMEM((16, 8, 128), F32),
            pltpu.VMEM((CH, 128), F32),
            pltpu.VMEM((CH, 128), F32),
            pltpu.VMEM((6, FRAMES, 32, 256), BF16),
            pltpu.VMEM((8, OWN, 128), BF16),
            pltpu.VMEM((CH, 128), BF16),
            dma((8,)),
            dma,
            dma((16, FRAMES)),
            dma,
            dma((16, FRAMES)),
            dma,
            dma((2, 8)),
            dma((4,)),
            dma((4,)),
            dma((2,)),
            dma((2,)),
            dma,
            dma,
            dma,
            dma,
        ],
        compiler_params=pltpu.CompilerParams(
            collective_id=0, has_side_effects=True, vmem_limit_bytes=48 << 20
        ),
        name="block",
    )(
        *[
            pltpu.with_memory_space_constraint(array, pltpu.HBM)
            for array in (
                latents.reshape(48, CH),
                first_gain,
                first_bias,
                second_gain,
                second_bias,
                first_kernel.reshape(27 * OWN, CH),
                second_kernel.reshape(27 * OWN, CH),
                expand_kernel,
            )
        ]
    ).reshape(3 * FRAMES, 2, 32, 512)


def solution(mesh):
    return jax.shard_map(
        shards,
        mesh=mesh,
        in_specs=(
            P("tm", "rows", None, None),
            P(),
            P(),
            P(),
            P(),
            P(None, None, None, "rows", None),
            P(None, None, None, "rows", None),
            P(None, "rows"),
        ),
        out_specs=P("tm", "rows", None, None),
        check_vma=False,
    )
```
